32 devices in a mesh: emb: 4 (over y, x), row: 4 (over z), phase: 2 (over core).
Axes of the slice: x: 2, y: 2, z: 4, core: 2. Of those that a mesh axis runs over, the one named last changes fastest.
Arguments:
- item_table: bfloat16 [4096, 512], P('emb'), may hold values from -10 to 10
- item_owner: int32 [4, 2, 1024, 1], P('emb', 'phase', 'row'), may hold values from 0 to 3; in each aligned block of 256 rows (0 to 255, 256 to 511, ..., all dimensions but the last counted through in order) at most 128 rows name the same one
- item_slot: int32 [4, 2, 1024], P('emb', 'phase', 'row'), may hold values from 0 to 1023
- seq_lengths: int32 [4, 2, 2], P('emb'), may hold values from 1 to 768, 1024 in all within a row
- row_grads: bfloat16 [4, 2, 1024, 512], P('emb', 'phase', 'row'), may hold values from -6 to 6
- proj_weight: bfloat16 [2, 512, 2048], P('phase'), may hold values from -2 to 2
- out_weight: bfloat16 [2, 512, 512], P('phase'), may hold values from -0.25 to 0.25
- final_gain: float32 [512], replicated, may hold values from 0.1 to 1.9
Outputs:
- sequence_states: bfloat16 [4, 2, 1024, 512], P('emb', 'phase', 'row')
- table_grad: float32 [4096, 512], P(('emb', 'row', 'phase'))
The draws below stay inside these ranges and needn't reach their ends.
Inputs may be any that keep to these rules, and one draw needn't show every extreme that they name: `item_owner`: among the 256 tokens of one device, at most 128 name the same owner, and in every draw some device has an owner named by exactly 128 of its tokens. `seq_lengths`: the 2 lengths of one micro-batch of one group sum to 1024; neither is longer than 768.
All inputs are finite; a program needn't handle non-finite values.
Results may differ from the reference program's by a relative error of at most 0.013.
Values may be sent and summed in bfloat16 or wider, within the bound.
No kernel may reach another device: no remote copies, remote signals or barrier semaphores. Data moves between devices by JAX's collectives and lax.ppermute only.
A program may use at most 64 MiB of HBM per device.

```python
import math
import jax
import jax.numpy as jnp
import numpy as np
from jax import lax

D = 512
HEADS = 4
HEAD_DIM = 128
V_DEV = 1024
TOK_DEV = 256
MICRO = 2
SEQS = 2
GROUP_TOK = 1024
MAXLEN = 768
CAP = 128
VOCAB = 4096
N_EMB = 4
N_PHASE = 2


def common_direction(key):
    raw_vector = jax.random.truncated_normal(jax.random.fold_in(key, 7), -4.0, 4.0, (D,), jnp.float32)
    return raw_vector / jnp.sqrt(jnp.sum(raw_vector * raw_vector))


def draw_item_table(key, part):
    direction = common_direction(key)
    noise_rows = jax.random.truncated_normal(jax.random.fold_in(key, 11), -4.0, 4.0, (VOCAB, D), jnp.float32)
    table_rows = math.sqrt(D) * direction[None, :] + noise_rows
    return jnp.clip(table_rows, -10.0, 10.0).astype(jnp.bfloat16)


def draw_proj_weight(key, part):
    direction = common_direction(key)
    columns = 4 * HEADS * HEAD_DIM
    inner_width = HEADS * HEAD_DIM
    base_draw = jax.random.truncated_normal(jax.random.fold_in(key, 13), -4.0, 4.0, (N_PHASE, D, columns), jnp.float32)
    along_dir = jnp.einsum('d,sdc->sc', direction, base_draw)
    base_perp = base_draw - direction[None, :, None] * along_dir[:, None, :]
    unit_scale = math.sqrt(2.0 / D)
    is_gate = jnp.arange(columns) < inner_width
    column_scale = jnp.where(is_gate, unit_scale, 2.0 * unit_scale)
    offsets = jnp.where(is_gate, 0.0, -2.0 * unit_scale)
    weights = base_perp * column_scale[None, None, :] + direction[None, :, None] * offsets[None, None, :]
    return jnp.clip(weights, -2.0, 2.0).astype(jnp.bfloat16)


def touch_ends(array, own_key, low, high):
    longest = array.shape.index(max(array.shape))
    spots = []
    for shift in (0, 1):
        where = [jax.random.randint(jax.random.fold_in(own_key, axis), (), 0, length) for axis, length in enumerate(array.shape)]
        where[longest] = (where[longest] + shift) % array.shape[longest]
        spots.append(tuple(where))
    return array.at[spots[0]].set(low).at[spots[1]].set(high)


def levels(own_key, dims, pieces, low, largest):
    loudness, own = 1.0, jax.random.fold_in(own_key, 6)
    for position, blocks in pieces:
        draws = jnp.exp(jax.random.uniform(jax.random.fold_in(own, position), (blocks,), jnp.float32, low / len(pieces), largest / len(pieces)))
        loudness = loudness * jnp.repeat(draws, dims[position] // blocks).reshape([-1 if axis == position else 1 for axis in range(len(dims))])
    return loudness


def rank_bounds(number_of, lean):
    weights = [(1 << 20) // math.isqrt(rank ** lean) + 1 for rank in range(1, number_of + 1)]
    deviation = 1 + sum(weights) // (1 << 30)
    return np.cumsum(np.array([max(1, weight // deviation) for weight in weights]))


def ranked(own_key, dims, count, slope):
    table = rank_bounds(count, slope)
    pick = jax.random.randint(jax.random.fold_in(own_key, 1), dims, 0, int(table[count - 1]))
    standing = jnp.searchsorted(jnp.asarray(table, jnp.int32), pick, side="right")
    return jax.random.permutation(jax.random.fold_in(own_key, 2), count)[standing].astype(jnp.int32)


def split_up(number_of, total, bound, slope):
    weights = [(1 << 20) // math.isqrt(rank ** slope) + 1 for rank in range(2, number_of + 1)]
    spare, given = total - bound - (number_of - 1), [1] * (number_of - 1)
    while spare > 0:
        free = [i for i in range(number_of - 1) if given[i] < bound]
        mass, remaining = sum([weights[i] for i in free]), spare
        for i in free:
            addition = min(bound - given[i], max(1, remaining * weights[i] // mass), spare)
            given[i] = given[i] + addition
            spare = spare - addition
    return np.array([bound] + given)


def uneven_parts(rng, number_of, total, most, lean):
    if number_of == 2:
        one = jax.random.randint(rng, (), max(1, total - most), min(most, total - 1) + 1)
        return jnp.stack([one, total - one])
    tallies = jnp.asarray(split_up(number_of, total, most, lean), jnp.int32)
    couples = (number_of - 1) // 2
    giver, sink = tallies[1:1 + 2 * couples:2], tallies[2:2 + 2 * couples:2]
    slack = jnp.minimum(giver - 1, most - sink)
    passed = jax.random.randint(jax.random.fold_in(rng, 1), (couples,), 0, 1 << 20) % (slack + 1)
    tallies = tallies.at[1:1 + 2 * couples:2].set(giver - passed).at[2:2 + 2 * couples:2].set(sink + passed)
    return tallies[jax.random.permutation(jax.random.fold_in(rng, 2), number_of)]


def deal_out(own_key, own, number, rows, count, top, reach, slope):
    sequence = jax.random.permutation(own_key, count)
    heavy_load, common = shares(count, rows * top, reach, slope, True), shares(count, rows * top, reach, slope, False)
    places = jnp.arange(count)

    def named(sizes, turn):
        used = int((sizes > 0).sum())
        fixed = max(1, used // 4)
        moved = fixed + (places - fixed + turn * (used - fixed)) % max(1, count - fixed)
        return jnp.zeros((count,), jnp.int32).at[sequence[jnp.where(places < fixed, places, moved)]].set(jnp.asarray(sizes, jnp.int32))

    sizes = jnp.where(number % 4 == 0, named(heavy_load, number // 4), named(common, number - number // 4 - 1))
    mixed = jax.random.permutation(jax.random.fold_in(own, 3), count)
    donor, taker = mixed[0:count // 2 * 2:2], mixed[1:count // 2 * 2:2]
    room = jnp.minimum(sizes[donor] - 1, reach - sizes[taker]) // 2
    room = jnp.where((donor == sequence[0]) | (taker == sequence[0]) | (sizes[taker] == 0), 0, jnp.maximum(room, 0))
    moved = jax.random.randint(jax.random.fold_in(own, 4), (count // 2,), 0, 1 << 20) % (room + 1)
    sizes = sizes.at[donor].add(-moved).at[taker].add(moved)
    members = jnp.searchsorted(jnp.cumsum(sizes), jnp.arange(rows * top), side="right").astype(jnp.int32)
    table = members.reshape(top, rows).T
    table = table[jax.random.permutation(jax.random.fold_in(own, 1), rows)]
    turn = jax.random.randint(jax.random.fold_in(own, 2), (rows, 1), 0, top)
    return jnp.take_along_axis(table, (jnp.arange(top)[None, :] + turn) % top, axis=1)


def shares(number_of, total, most, skew, full):
    portions = [(1 << 20) // math.isqrt(rank ** skew) + 1 for rank in range(1, number_of + 1)]
    largest = most if full else min(most, max(-(-total // number_of), total * portions[0] // sum(portions)))
    least = 1 if total - largest >= number_of - 1 else 0
    given, rest = [largest] + [least] * (number_of - 1), total - largest - least * (number_of - 1)
    while rest > 0:
        movable = [i for i in range(1, number_of) if given[i] < largest] or [i for i in range(1, number_of) if given[i] < most]
        pool, budget = sum([portions[i] for i in movable]), rest
        for i in movable:
            more = min(most - given[i], max(1, budget * portions[i] // pool), rest)
            given[i] = given[i] + more
            rest = rest - more
    return np.array(given)


def centred(key, dims, deviation, bound, cuts=(), kind=jnp.bfloat16):
    result = jax.random.normal(key, dims, jnp.float32) * deviation
    if len(cuts) > 0:
        result = levels(key, dims, cuts, -0.22, 0.18) * result
    return jnp.clip(result, min=-bound, max=bound).astype(kind)


def setup_inputs(seed: int = 0) -> dict:
    streams_of = jax.random.split(jax.random.key(seed), 9)
    item_table = draw_item_table(jax.random.fold_in(streams_of[8], 71), 0)
    item_owner_keys = jax.random.split(jax.random.fold_in(streams_of[1], 1), N_EMB * MICRO * GROUP_TOK // TOK_DEV)
    item_owner_turns = jax.random.permutation(jax.random.fold_in(streams_of[1], 3), N_EMB * MICRO * GROUP_TOK // TOK_DEV)
    item_owner = jax.vmap(lambda own, number: deal_out(jax.random.fold_in(streams_of[1], 2), own, number, TOK_DEV, N_EMB, 1, CAP, 2))(item_owner_keys, item_owner_turns).reshape((N_EMB, MICRO, GROUP_TOK, 1))
    item_slot = touch_ends(ranked(streams_of[2], (N_EMB, MICRO, GROUP_TOK), V_DEV, 2), jax.random.fold_in(streams_of[2], 3), 0, V_DEV - 1).astype(jnp.int32)
    seq_lengths = jax.vmap(lambda own: uneven_parts(own, SEQS, GROUP_TOK, MAXLEN, 0))(jax.random.split(streams_of[3], N_EMB * MICRO)).reshape((N_EMB, MICRO, SEQS)).astype(jnp.int32)
    row_grads = centred(streams_of[4], (N_EMB, MICRO, GROUP_TOK, D), 1.0, 6.0, ((0, 4), (1, 2), (2, 4)))
    proj_weight = draw_proj_weight(jax.random.fold_in(streams_of[8], 71), 0)
    out_weight = centred(streams_of[6], (N_PHASE, HEADS * HEAD_DIM, D), (HEADS * HEAD_DIM) ** -0.5, 0.25, ((0, 2),))
    final_gain = jnp.clip(1.0 + 0.18 * jax.random.normal(streams_of[7], (D,), jnp.float32), 0.1, 1.9)
    return {"item_table": item_table, "item_owner": item_owner, "item_slot": item_slot, "seq_lengths": seq_lengths, "row_grads": row_grads, "proj_weight": proj_weight, "out_weight": out_weight, "final_gain": final_gain}


norm_eps = 1e-05

def layer_norm(values):
    average = lax.optimization_barrier(jnp.mean(values, axis=-1, keepdims=True))
    centered = values - average
    return centered * lax.rsqrt(lax.optimization_barrier(jnp.mean(centered * centered, axis=-1, keepdims=True)) + norm_eps)

def segment_of(positions, lengths):
    bounds = jnp.cumsum(lengths.astype(jnp.int32)).astype(jnp.int32)[:-1]
    return lax.optimization_barrier(jnp.sum((positions[:, None] >= bounds[None, :]).astype(jnp.int32), axis=1))

def section(inputs, proj_w, out_w, lengths):
    normed = layer_norm(inputs.astype(jnp.float32)).astype(jnp.bfloat16)
    activated = jax.nn.silu(jnp.dot(normed, proj_w, preferred_element_type=jnp.float32)).astype(jnp.bfloat16)
    inner_width = HEADS * HEAD_DIM
    gate_rows = activated[:, :inner_width]
    value_rows = activated[:, inner_width:2 * inner_width]
    query_rows = activated[:, 2 * inner_width:3 * inner_width]
    key_rows = activated[:, 3 * inner_width:]
    positions = jnp.arange(GROUP_TOK, dtype=jnp.int32)
    segments = segment_of(positions, lengths)
    visible = (positions[None, :] <= positions[:, None]) & (segments[None, :] == segments[:, None])
    query_heads = query_rows.reshape(GROUP_TOK, HEADS, HEAD_DIM).astype(jnp.float32)
    key_heads = key_rows.reshape(GROUP_TOK, HEADS, HEAD_DIM).astype(jnp.float32)
    value_heads = value_rows.reshape(GROUP_TOK, HEADS, HEAD_DIM).astype(jnp.float32)
    scores = jnp.einsum('qhd,khd->hqk', query_heads, key_heads)
    attn_weights = jnp.where(visible[None], jax.nn.silu(scores), 0.0).astype(jnp.bfloat16)
    mixed_heads = jnp.einsum('hqk,khd->qhd', attn_weights.astype(jnp.float32), value_heads).reshape(GROUP_TOK, inner_width)
    gated = (layer_norm(mixed_heads) * gate_rows.astype(jnp.float32)).astype(jnp.bfloat16)
    return inputs.astype(jnp.float32) + jnp.dot(gated, out_w, preferred_element_type=jnp.float32)

def reference(item_table, item_owner, item_slot, seq_lengths, row_grads, proj_weight, out_weight, final_gain):
    item_rows = (item_owner[..., 0] * V_DEV + item_slot).astype(jnp.int32)
    embedded = item_table[item_rows]

    def per_group(packed):
        group_rows, group_lengths = packed
        states = []
        for micro in range(MICRO):
            middle = section(group_rows[micro], proj_weight[0], out_weight[0], group_lengths[micro]).astype(jnp.bfloat16)
            closing = section(middle, proj_weight[1], out_weight[1], group_lengths[micro])
            states.append((layer_norm(closing) * final_gain).astype(jnp.bfloat16))
        return jnp.stack(states)
    sequence_states = lax.map(per_group, (embedded, seq_lengths))
    table_grad = jnp.zeros((VOCAB, D), jnp.float32).at[item_rows.reshape(-1)].add(row_grads.reshape(-1, D).astype(jnp.float32))
    return (sequence_states, table_grad)
```

```python
import functools

import jax
import jax.numpy as jnp
from jax import lax
from jax.experimental import pallas as pl
from jax.experimental.pallas import tpu as pltpu
from jax.sharding import PartitionSpec as P

HEADS = 4
HEAD_DIM = 128
INNER = HEADS * HEAD_DIM
SLOT_BASE = 128

norm_eps = 1e-05

NT = (((1,), (1,)), ((), ()))


def exchanged(shard, axis, by):
    count = lax.axis_size(axis)
    return lax.ppermute(shard, axis, [(i, i ^ by) for i in range(count)])


def layer_norm(values):
    average = jnp.mean(values, axis=-1, keepdims=True)
    centered = values - average
    return centered * lax.rsqrt(jnp.mean(centered * centered, axis=-1, keepdims=True) + norm_eps)


def silu(values):
    half = 0.5 * values
    return half * jnp.tanh(half) + half


def dot(left, right):
    return jnp.dot(left, right, preferred_element_type=jnp.float32)


def as_column(row):
    count = row.shape[1]
    down = lax.broadcasted_iota(jnp.int32, (count, count), 0)
    along = lax.broadcasted_iota(jnp.int32, (count, count), 1)
    picked = jnp.where(down == along, jnp.broadcast_to(row, (count, count)), 0.0)
    return jnp.sum(picked, axis=1, keepdims=True)


def pack_kernel(parties, capacity, owner_ref, slot_ref, grad_ref, *packed_refs):
    owner = owner_ref[...]
    slot = slot_ref[...]
    count = owner.shape[1]
    before = (
        lax.broadcasted_iota(jnp.int32, (count, count), 0)
        < lax.broadcasted_iota(jnp.int32, (count, count), 1)
    ).astype(jnp.bfloat16)
    high = slot // SLOT_BASE
    low = slot - high * SLOT_BASE
    line = lax.broadcasted_iota(jnp.int32, (16, count), 0)
    codes = jnp.where(line == 0, high + 1, jnp.where(line == 1, low, 0))
    codes = codes.astype(jnp.float32).astype(jnp.bfloat16)
    place = lax.broadcasted_iota(jnp.int32, (capacity, count), 0)
    for party in range(parties):
        named = owner == party
        flags = jnp.broadcast_to(named, (16, count)).astype(jnp.float32).astype(jnp.bfloat16)
        rank = dot(flags, before)[0:1].astype(jnp.int32)
        chosen = (named & (rank == place)).astype(jnp.float32).astype(jnp.bfloat16)
        packed_refs[party][0:capacity, :] = dot(chosen, grad_ref[...]).astype(jnp.bfloat16)
        sent_codes = lax.dot_general(codes, chosen, NT, preferred_element_type=jnp.float32)
        packed_refs[party][capacity : capacity + 16, 0:capacity] = sent_codes.astype(jnp.bfloat16)


def scatter_kernel(parties, capacity, row_ids, place_ref, *refs):
    arrived = refs[:parties]
    keep_ref, send_ref = refs[parties:]
    rows, phases = row_ids
    my_row, my_phase = place_ref[0], place_ref[1]
    block = keep_ref.shape[0] // rows
    values = jnp.concatenate([ref[0:capacity, :] for ref in arrived], axis=0)
    slots = []
    for ref in arrived:
        codes = ref[capacity : capacity + 16, 0:capacity].astype(jnp.float32)
        slots.append((codes[0:1] - 1.0) * SLOT_BASE + codes[1:2])
    slots = jnp.concatenate(slots, axis=1).astype(jnp.int32)
    down = lax.broadcasted_iota(jnp.int32, (block, parties * capacity), 0)
    for other in range(phases):
        for step in range(rows):
            base = ((my_row ^ step) * phases + (my_phase ^ other)) * block
            chosen = (slots - base == down).astype(jnp.float32).astype(jnp.bfloat16)
            total = dot(chosen, values)
            if other == 0:
                keep_ref[step * block : (step + 1) * block, :] = total
            else:
                send_ref[step * block : (step + 1) * block, :] = total.astype(jnp.bfloat16)


def loop(count, body):
    if count <= 4:
        for index in range(count):
            body(index)
    else:
        lax.fori_loop(0, count, lambda index, carry: (body(index), carry)[1], 0)


def section_kernel(
    window,
    place_ref,
    lengths_ref,
    ids_ref,
    table_ref,
    near_ref,
    next_ref,
    far_ref,
    near2_ref,
    next2_ref,
    far2_ref,
    proj_own,
    proj_other,
    outw_own,
    outw_other,
    gain_ref,
    out_ref,
    proj_ref,
    outw_ref,
    emb_ref,
    act_ref,
    mid_ref,
    mix_ref,
    sems,
):
    my_row, my_phase = place_ref[0], place_ref[1]
    size = out_ref.shape[0]
    half = near_ref.shape[0]
    owned = 2 * half
    copies = [
        pltpu.make_async_copy(proj_own.at[0], proj_ref.at[my_phase], sems.at[0]),
        pltpu.make_async_copy(proj_other.at[0], proj_ref.at[1 - my_phase], sems.at[1]),
        pltpu.make_async_copy(outw_own.at[0], outw_ref.at[my_phase], sems.at[2]),
        pltpu.make_async_copy(outw_other.at[0], outw_ref.at[1 - my_phase], sems.at[3]),
    ]
    for copy in copies:
        copy.start()

    def rows(block):
        if isinstance(block, int):
            return pl.ds(block * size, size)
        return pl.ds(pl.multiple_of(block * size, size), size)

    along = lax.broadcasted_iota(jnp.int32, (size, half), 1)
    mine = pl.ds(pl.multiple_of(my_phase * half, half), half)
    theirs = pl.ds(pl.multiple_of((1 - my_phase) * half, half), half)

    def look_up(block):
        ids = as_column(ids_ref[pl.ds(block, 1), :].astype(jnp.float32)).astype(jnp.int32)
        total = jnp.zeros((size, emb_ref.shape[1]), jnp.float32)
        pieces = (
            (0, table_ref, mine),
            (half, table_ref, theirs),
            (owned, near_ref, None),
            (owned + half, next2_ref, None),
            (2 * owned, next_ref, None),
            (2 * owned + half, near2_ref, None),
            (3 * owned, far_ref, None),
            (3 * owned + half, far2_ref, None),
        )
        for base, piece, part in pieces:
            chosen = (along == ids - base).astype(jnp.float32).astype(jnp.bfloat16)
            total += dot(chosen, piece[...] if part is None else piece[part, :])
        emb_ref[rows(block), :] = total

    loop(window, look_up)
    for copy in copies:
        copy.wait()

    first_pos = (my_row - (window - 1)) * size
    down = lax.broadcasted_iota(jnp.int32, (size, 1), 0)
    across = lax.broadcasted_iota(jnp.int32, (1, size), 1)

    def mixed_of(block):
        query_pos = first_pos + block * size + down
        start = jnp.zeros((size, 1), jnp.int32)
        bound = jnp.int32(0)
        for index in range(lengths_ref.shape[2] - 1):
            bound = bound + lengths_ref[0, my_phase, index]
            start = jnp.where(query_pos >= bound, bound, start)

        def piece(key_block, diagonal):
            key_pos = first_pos + key_block * size + across
            visible = key_pos >= start
            if diagonal:
                visible = visible & (key_pos <= query_pos)
            for head in range(HEADS):
                cols = head * HEAD_DIM
                queries = act_ref[rows(block), 2 * INNER + cols : 2 * INNER + cols + HEAD_DIM]
                keys = act_ref[rows(key_block), 3 * INNER + cols : 3 * INNER + cols + HEAD_DIM]
                values = act_ref[rows(key_block), INNER + cols : INNER + cols + HEAD_DIM]
                scores = lax.dot_general(queries, keys, NT, preferred_element_type=jnp.float32)
                weights = jnp.where(visible, silu(scores), 0.0).astype(jnp.bfloat16)
                update = dot(weights, values)
                if diagonal:
                    mix_ref[:, cols : cols + HEAD_DIM] = update
                else:
                    mix_ref[:, cols : cols + HEAD_DIM] += update

        piece(block, True)
        if isinstance(block, int):
            loop(block, lambda key_block: piece(key_block, False))
        else:
            lax.fori_loop(0, block, lambda key_block, c: (piece(key_block, False), c)[1], 0)
        return mix_ref[...]

    def branch(block, section):
        gates = act_ref[rows(block), 0:INNER].astype(jnp.float32)
        gated = (layer_norm(mixed_of(block)) * gates).astype(jnp.bfloat16)
        return dot(gated, outw_ref[section])

    def first_section(block):
        values = emb_ref[rows(block), :]
        normed = layer_norm(values).astype(jnp.bfloat16)
        act_ref[rows(block), :] = silu(dot(normed, proj_ref[0])).astype(jnp.bfloat16)
        mid_ref[rows(block), :] = (values + branch(block, 0)).astype(jnp.bfloat16)

    loop(window, first_section)

    def second_inputs(block):
        normed = layer_norm(mid_ref[rows(block), :].astype(jnp.float32)).astype(jnp.bfloat16)
        for cols in (INNER, 3 * INNER):
            act = silu(dot(normed, proj_ref[1, :, cols : cols + INNER]))
            act_ref[rows(block), cols : cols + INNER] = act.astype(jnp.bfloat16)
        return normed

    if window > 1:
        loop(window - 1, second_inputs)
    last = window - 1
    normed = second_inputs(last)
    for cols in (0, 2 * INNER):
        act = silu(dot(normed, proj_ref[1, :, cols : cols + INNER]))
        act_ref[rows(last), cols : cols + INNER] = act.astype(jnp.bfloat16)
    closing = mid_ref[rows(last), :].astype(jnp.float32) + branch(last, 1)
    out_ref[...] = (layer_norm(closing) * gain_ref[...]).astype(jnp.bfloat16)


def body(
    item_table, item_owner, item_slot, seq_lengths, row_grads, proj_weight, out_weight, final_gain
):
    parties = lax.axis_size("emb")
    row_count = lax.axis_size("row")
    phases = lax.axis_size("phase")
    my_emb = lax.axis_index("emb")
    my_row = lax.axis_index("row")
    my_phase = lax.axis_index("phase")
    size = item_slot.shape[2]
    width = item_table.shape[1]
    owned = item_table.shape[0]
    half = owned // 2
    capacity = max(16, 2 * size // parties)
    window = -(-3 * row_count // 4)
    vmem = pltpu.MemorySpace.VMEM
    smem = pltpu.MemorySpace.SMEM
    params = pltpu.CompilerParams(vmem_limit_bytes=48 * 1024 * 1024)

    def across(shard, first):
        pairs = []
        for emb in range(parties):
            for phase in range(phases):
                by = 1 if (phase == 0) == first else 2
                pairs.append((emb * phases + phase, (emb ^ by) * phases + phase))
        return lax.ppermute(shard, ("emb", "phase"), pairs)

    own_half = lax.dynamic_slice_in_dim(item_table, my_phase * half, half, 0)
    near = across(own_half, True)
    following = across(own_half, False)
    far = across(near, False)
    near2 = exchanged(near, "phase", 1)
    next2 = exchanged(following, "phase", 1)
    far2 = exchanged(far, "phase", 1)

    owner = item_owner.reshape(1, size)
    slot = item_slot.reshape(1, size)
    nearby = owner ^ my_emb
    swapped = (nearby // 2) | ((nearby % 2) * 2)
    turned = jnp.where(my_phase == 0, nearby, swapped)
    ids = turned * owned + (slot ^ (my_phase * half))
    window_ids = [ids]
    for step in range(1, window):
        pairs = [(i, i + step) for i in range(row_count - step)]
        arrived_ids = lax.ppermute(ids, "row", pairs)
        window_ids.insert(0, jnp.where(my_row >= step, arrived_ids, -1))
    window_ids = jnp.concatenate(window_ids, axis=0)

    proj_other = exchanged(proj_weight, "phase", 1)
    outw_other = exchanged(out_weight, "phase", 1)

    packed = pl.pallas_call(
        functools.partial(pack_kernel, parties, capacity),
        out_shape=[jax.ShapeDtypeStruct((capacity + 16, width), jnp.bfloat16)] * parties,
        in_specs=[pl.BlockSpec(memory_space=vmem)] * 3,
        out_specs=[pl.BlockSpec(memory_space=vmem)] * parties,
        compiler_params=params,
        name="pack",
    )(nearby, slot, row_grads.reshape(size, width))
    arrived = [packed[0]] + [exchanged(packed[by], "emb", by) for by in range(1, parties)]
    place = jnp.stack([my_row, my_phase]).astype(jnp.int32)
    block = owned // (row_count * phases)
    keep, send = pl.pallas_call(
        functools.partial(scatter_kernel, parties, capacity, (row_count, phases)),
        out_shape=[
            jax.ShapeDtypeStruct((row_count * block, width), jnp.float32),
            jax.ShapeDtypeStruct((row_count * block, width), jnp.bfloat16),
        ],
        in_specs=[pl.BlockSpec(memory_space=smem)] + [pl.BlockSpec(memory_space=vmem)] * parties,
        out_specs=[pl.BlockSpec(memory_space=vmem)] * 2,
        compiler_params=params,
        name="scatter",
    )(place, *arrived)
    total = keep + exchanged(send, "phase", 1).astype(jnp.float32)
    by = 1
    while by < row_count:
        total = total.reshape(-1, 2, block, width)
        sent = total[:, 1].astype(jnp.bfloat16)
        total = total[:, 0] + exchanged(sent, "row", by).astype(jnp.float32)
        by *= 2
    table_grad = total.reshape(block, width)

    hbm = pl.ANY
    states = pl.pallas_call(
        functools.partial(section_kernel, window),
        out_shape=jax.ShapeDtypeStruct((size, width), jnp.bfloat16),
        in_specs=[pl.BlockSpec(memory_space=smem)] * 2
        + [pl.BlockSpec(memory_space=vmem)] * 8
        + [pl.BlockSpec(memory_space=hbm)] * 4
        + [pl.BlockSpec(memory_space=vmem)],
        out_specs=pl.BlockSpec(memory_space=vmem),
        scratch_shapes=[
            pltpu.VMEM((2,) + proj_weight.shape[1:], jnp.bfloat16),
            pltpu.VMEM((2,) + out_weight.shape[1:], jnp.bfloat16),
            pltpu.VMEM((window * size, width), jnp.float32),
            pltpu.VMEM((window * size, 4 * INNER), jnp.bfloat16),
            pltpu.VMEM((window * size, width), jnp.bfloat16),
            pltpu.VMEM((size, INNER), jnp.float32),
            pltpu.SemaphoreType.DMA((4,)),
        ],
        compiler_params=params,
        name="sections",
    )(
        place,
        seq_lengths,
        window_ids,
        item_table,
        near,
        following,
        far,
        near2,
        next2,
        far2,
        proj_weight,
        proj_other,
        out_weight,
        outw_other,
        final_gain.reshape(1, width),
    )
    return (states.reshape(1, 1, size, width), table_grad)


def solution(mesh):
    placed = (
        P("emb", None),
        P("emb", "phase", "row", None),
        P("emb", "phase", "row"),
        P("emb", None, None),
        P("emb", "phase", "row", None),
        P("phase", None, None),
        P("phase", None, None),
        P(),
    )
    return jax.shard_map(
        body,
        mesh=mesh,
        in_specs=placed,
        out_specs=(P("emb", "phase", "row", None), P(("emb", "row", "phase"), None)),
        check_vma=False,
    )
```

```python
import functools

import jax
import jax.numpy as jnp
from jax import lax
from jax.experimental import pallas as pl
from jax.experimental.pallas import tpu as pltpu
from jax.sharding import PartitionSpec as P

HEADS = 4
HEAD_DIM = 128
INNER = HEADS * HEAD_DIM
SLOT_BASE = 128
CODE_ROWS = 16

norm_eps = 1e-05

NT = (((1,), (1,)), ((), ()))


def exchanged(shard, axis, by):
    count = lax.axis_size(axis)
    return lax.ppermute(shard, axis, [(i, i ^ by) for i in range(count)])


def layer_norm(values):
    average = jnp.mean(values, axis=-1, keepdims=True)
    centered = values - average
    return centered * lax.rsqrt(jnp.mean(centered * centered, axis=-1, keepdims=True) + norm_eps)


def silu(values):
    half = 0.5 * values
    return half * jnp.tanh(half) + half


def dot(left, right):
    return jnp.dot(left, right, preferred_element_type=jnp.float32)


def as_column(row):
    count = row.shape[1]
    down = lax.broadcasted_iota(jnp.int32, (count, count), 0)
    along = lax.broadcasted_iota(jnp.int32, (count, count), 1)
    picked = jnp.where(down == along, jnp.broadcast_to(row, (count, count)), 0.0)
    return jnp.sum(picked, axis=1, keepdims=True)


def coded(numbers):
    high = numbers // SLOT_BASE
    low = numbers - high * SLOT_BASE
    line = lax.broadcasted_iota(jnp.int32, (CODE_ROWS, numbers.shape[1]), 0)
    codes = jnp.where(line == 0, high, jnp.where(line == 1, low, 0)).astype(jnp.float32)
    return codes.astype(jnp.bfloat16)


def decoded(codes):
    codes = codes.astype(jnp.float32)
    return codes[0:1] * SLOT_BASE + codes[1:2]


def pack_kernel(
    parties, capacity, owned, place_ref, owner_ref, slot_ref, grad_ref, *packed_refs
):
    ids_ref = packed_refs[parties]
    my_phase = place_ref[1]
    owner = owner_ref[...] ^ place_ref[2]
    slot = slot_ref[...]
    count = owner.shape[1]
    width = grad_ref.shape[1]
    half = owned // 2
    swapped = (owner // 2) | ((owner % 2) * 2)
    turned = jnp.where(my_phase == 0, owner, swapped)
    moved = slot + my_phase * half
    moved = jnp.where(moved >= owned, moved - owned, moved)
    ids_ref[...] = turned * owned + jnp.where(turned == 3, moved, slot)
    before = (
        lax.broadcasted_iota(jnp.int32, (count, count), 0)
        < lax.broadcasted_iota(jnp.int32, (count, count), 1)
    ).astype(jnp.bfloat16)
    codes = coded(slot + SLOT_BASE)
    place = lax.broadcasted_iota(jnp.int32, (capacity, count), 0)
    chosen = []
    for party in range(parties):
        named = owner == party
        flags = jnp.broadcast_to(named, (CODE_ROWS, count)).astype(jnp.float32)
        rank = dot(flags.astype(jnp.bfloat16), before)[0:1].astype(jnp.int32)
        picks = (named & (rank == place)).astype(jnp.float32).astype(jnp.bfloat16)
        chosen.append(picks)
        sent = lax.dot_general(codes, picks, NT, preferred_element_type=jnp.float32)
        packed_refs[party][capacity : capacity + CODE_ROWS, :] = jnp.concatenate(
            [sent, jnp.zeros((CODE_ROWS, width - capacity), jnp.float32)], axis=1
        ).astype(jnp.bfloat16)
    for party in range(parties):
        rows = dot(chosen[party], grad_ref[...])
        packed_refs[party][0:capacity, :] = rows.astype(jnp.bfloat16)


def scatter_kernel(parties, capacity, row_ids, place_ref, *refs):
    arrived = refs[:parties]
    keep_ref, send_ref = refs[parties:]
    rows, phases = row_ids
    my_row, my_phase = place_ref[0], place_ref[1]
    block = keep_ref.shape[0] // rows
    values = jnp.concatenate([ref[0:capacity, :] for ref in arrived], axis=0)
    slots = [
        decoded(ref[capacity : capacity + CODE_ROWS, 0:capacity]) - SLOT_BASE for ref in arrived
    ]
    slots = jnp.concatenate(slots, axis=1).astype(jnp.int32)
    down = lax.broadcasted_iota(jnp.int32, (block, parties * capacity), 0)
    for other in range(phases):
        for step in range(rows):
            base = ((my_row ^ step) * phases + (my_phase ^ other)) * block
            chosen = (slots - base == down).astype(jnp.float32).astype(jnp.bfloat16)
            total = dot(chosen, values)
            if other == 0:
                keep_ref[step * block : (step + 1) * block, :] = total
            else:
                send_ref[step * block : (step + 1) * block, :] = total.astype(jnp.bfloat16)


def combine_kernel(block, kept_ref, come_ref, own_ref, *sent_refs):
    for step in range(len(sent_refs) + 1):
        part = slice(step * block, (step + 1) * block)
        total = kept_ref[part, :] + come_ref[part, :].astype(jnp.float32)
        if step == 0:
            own_ref[...] = total
        else:
            sent_refs[step - 1][...] = total.astype(jnp.bfloat16)


def finish_kernel(own_ref, *refs):
    total = own_ref[...]
    for come_ref in refs[:-1]:
        total = total + come_ref[...].astype(jnp.float32)
    refs[-1][...] = total


def loop(count, body):
    if count <= 4:
        for index in range(count):
            body(index)
    else:
        lax.fori_loop(0, count, lambda index, carry: (body(index), carry)[1], 0)


def rows_at(start, count, step):
    if isinstance(start, int):
        return pl.ds(start, count)
    return pl.ds(pl.multiple_of(start, step), count)


def tall_blocks(window):
    return window if window <= 4 else 1


def look_up(ids, pieces):
    total = None
    for base, piece in pieces:
        along = lax.broadcasted_iota(jnp.int32, (ids.shape[0], piece.shape[0]), 1)
        chosen = (along == ids - base).astype(jnp.float32).astype(jnp.bfloat16)
        part = dot(chosen, piece[...])
        total = part if total is None else total + part
    return total


def lookup_kernel(window, place_ref, ids_ref, table_ref, near_ref, next_ref, emb_ref, column_ref):
    my_row = place_ref[0]
    size = ids_ref.shape[1]
    owned = table_ref.shape[0]

    def column(index):
        row = my_row - (window - 1) + index
        ids = ids_ref[pl.ds(jnp.maximum(row, 0) ^ my_row, 1), :].astype(jnp.float32)
        return as_column(jnp.where(row >= 0, ids, -1.0))

    tall = tall_blocks(window)
    height = tall * size
    pieces = ((0, table_ref), (owned, near_ref), (2 * owned, next_ref))

    def step(index):
        ids = [column(index * tall + part) for part in range(tall)]
        ids = jnp.concatenate(ids, axis=0).astype(jnp.int32)
        emb_ref[rows_at(index * height, height, size), :] = look_up(ids, pieces)
        column_ref[rows_at(index * height, height, size), :] = ids - 3 * owned

    loop(window // tall, step)


def section_kernel(
    window,
    place_ref,
    lengths_ref,
    ids_ref,
    early_ref,
    far_ref,
    far2_ref,
    proj_own,
    proj_other,
    outw_own,
    outw_other,
    gain_ref,
    out_ref,
    proj_ref,
    outw_ref,
    emb_ref,
    act_ref,
    mid_ref,
    mix_ref,
    sems,
):
    my_row, my_phase = place_ref[0], place_ref[1]
    size = out_ref.shape[0]
    half = far_ref.shape[0]
    copies = [
        pltpu.make_async_copy(proj_own.at[0], proj_ref.at[my_phase], sems.at[0]),
        pltpu.make_async_copy(proj_other.at[0], proj_ref.at[1 - my_phase], sems.at[1]),
        pltpu.make_async_copy(outw_own.at[0], outw_ref.at[my_phase], sems.at[2]),
        pltpu.make_async_copy(outw_other.at[0], outw_ref.at[1 - my_phase], sems.at[3]),
    ]
    for copy in copies:
        copy.start()

    tall = tall_blocks(window)
    height = tall * size

    def rows(start, count=height):
        return rows_at(start, count, size)

    def late(step):
        part = rows(step * height)
        found = look_up(ids_ref[part, :], ((0, far_ref), (half, far2_ref)))
        emb_ref[part, :] = early_ref[part, :] + found

    loop(window // tall, late)
    copies[0].wait()
    copies[1].wait()

    first_pos = (my_row - (window - 1)) * size
    across = lax.broadcasted_iota(jnp.int32, (1, size), 1)

    def attend(start, count, key_start, diagonal):
        query_pos = first_pos + start + lax.broadcasted_iota(jnp.int32, (count, 1), 0)
        key_pos = first_pos + key_start + across
        earliest = jnp.zeros((count, 1), jnp.int32)
        bound = jnp.int32(0)
        for index in range(lengths_ref.shape[2] - 1):
            bound = bound + lengths_ref[0, my_phase, index]
            earliest = jnp.where(query_pos >= bound, bound, earliest)
        visible = key_pos >= earliest
        if diagonal:
            visible = visible & (key_pos <= query_pos)
        for head in range(HEADS):
            cols = head * HEAD_DIM
            queries = act_ref[rows(start, count), 2 * INNER + cols : 2 * INNER + cols + HEAD_DIM]
            keys = act_ref[rows(key_start, size), 3 * INNER + cols : 3 * INNER + cols + HEAD_DIM]
            values = act_ref[rows(key_start, size), INNER + cols : INNER + cols + HEAD_DIM]
            scores = lax.dot_general(queries, keys, NT, preferred_element_type=jnp.float32)
            weights = jnp.where(visible, silu(scores), 0.0).astype(jnp.bfloat16)
            mix_ref[rows(start, count), cols : cols + HEAD_DIM] += dot(weights, values)

    def project(start, count, section, parts):
        source = emb_ref if section == 0 else mid_ref
        values = source[rows(start, count), :].astype(jnp.float32)
        normed = layer_norm(values).astype(jnp.bfloat16)
        for part in parts:
            cols = part * INNER
            act = silu(dot(normed, proj_ref[section, :, cols : cols + INNER]))
            act_ref[rows(start, count), cols : cols + INNER] = act.astype(jnp.bfloat16)

    def finish(start, count, section):
        source = emb_ref if section == 0 else mid_ref
        values = source[rows(start, count), :].astype(jnp.float32)
        gates = act_ref[rows(start, count), 0:INNER].astype(jnp.float32)
        gated = (layer_norm(mix_ref[rows(start, count), :]) * gates).astype(jnp.bfloat16)
        return values + dot(gated, outw_ref[section])

    last = (window - 1) * size
    mix_ref[...] = jnp.zeros(mix_ref.shape, jnp.float32)
    loop(window // tall, lambda step: project(step * height, height, 0, (3, 2, 1, 0)))
    if tall == window:
        for block in range(window):
            attend(block * size, height - block * size, block * size, True)
    else:

        def with_keys(block):
            attend(block * size, size, block * size, True)
            lax.fori_loop(
                block + 1,
                window,
                lambda later, c: (attend(later * size, size, block * size, False), c)[1],
                0,
            )

        loop(window, with_keys)

    copies[2].wait()
    copies[3].wait()

    def close_first(step):
        mid_ref[rows(step * height), :] = finish(step * height, height, 0).astype(jnp.bfloat16)

    loop(window // tall, close_first)
    mix_ref[last : last + size, :] = jnp.zeros((size, INNER), jnp.float32)
    loop(window // tall, lambda step: project(step * height, height, 1, (3, 1)))
    project(last, size, 1, (2, 0))
    attend(last, size, last, True)
    loop(window - 1, lambda block: attend(last, size, block * size, False))
    closing = finish(last, size, 1)
    out_ref[...] = (layer_norm(closing) * gain_ref[...]).astype(jnp.bfloat16)


def body(
    item_table, item_owner, item_slot, seq_lengths, row_grads, proj_weight, out_weight, final_gain
):
    parties = lax.axis_size("emb")
    row_count = lax.axis_size("row")
    phases = lax.axis_size("phase")
    my_emb = lax.axis_index("emb")
    my_row = lax.axis_index("row")
    my_phase = lax.axis_index("phase")
    size = item_slot.shape[2]
    width = item_table.shape[1]
    owned = item_table.shape[0]
    half = owned // 2
    capacity = max(16, 2 * size // parties)
    window = -(-3 * row_count // 4)
    vmem = pltpu.MemorySpace.VMEM
    smem = pltpu.MemorySpace.SMEM

    def params(mebibytes):
        return pltpu.CompilerParams(vmem_limit_bytes=mebibytes * 1024 * 1024)

    def cost(products):
        return pl.CostEstimate(flops=2 * products, bytes_accessed=0, transcendentals=0)

    def across(shard, first):
        pairs = []
        for emb in range(parties):
            for phase in range(phases):
                by = 1 if (phase == 0) == first else 2
                pairs.append((emb * phases + phase, (emb ^ by) * phases + phase))
        return lax.ppermute(shard, ("emb", "phase"), pairs)

    place = jnp.stack([my_row, my_phase, my_emb]).astype(jnp.int32)
    proj_other = exchanged(proj_weight, "phase", 1)
    outw_other = exchanged(out_weight, "phase", 1)

    on_chip = pl.BlockSpec(memory_space=vmem)
    scalars = pl.BlockSpec(memory_space=smem)
    anywhere = pl.BlockSpec(memory_space=pl.ANY)

    def array(rows, dtype=jnp.bfloat16):
        return jax.ShapeDtypeStruct((rows, width), dtype)

    *packed, ids = pl.pallas_call(
        functools.partial(pack_kernel, parties, capacity, owned),
        out_shape=[array(capacity + CODE_ROWS)] * parties
        + [jax.ShapeDtypeStruct((1, size), jnp.int32)],
        in_specs=[scalars] + [on_chip] * 3,
        out_specs=[on_chip] * (parties + 1),
        compiler_params=params(8),
        name="pack",
    )(place, item_owner.reshape(1, size), item_slot.reshape(1, size), row_grads.reshape(size, width))
    arrived = [packed[0]] + [exchanged(packed[by], "emb", by) for by in range(1, parties)]
    by = 1
    while by < row_count:
        ids = jnp.concatenate([ids, exchanged(ids, "row", by)], axis=0)
        by *= 2
    near = across(item_table, True)
    near, ids, *arrived = lax.optimization_barrier((near, ids, *arrived))
    following = exchanged(near, "phase", 1)
    far = across(lax.dynamic_slice_in_dim(near, my_phase * half, half, 0), False)
    block = owned // (row_count * phases)
    count = row_count * block
    kept, sent = pl.pallas_call(
        functools.partial(scatter_kernel, parties, capacity, (row_count, phases)),
        out_shape=[array(count, jnp.float32), array(count)],
        in_specs=[scalars] + [on_chip] * parties,
        out_specs=[on_chip] * 2,
        compiler_params=params(8),
        name="scatter",
    )(place, *arrived)
    come = exchanged(sent, "phase", 1)
    own, *sent = pl.pallas_call(
        functools.partial(combine_kernel, block),
        out_shape=[array(block, jnp.float32)] + [array(block)] * (row_count - 1),
        in_specs=[on_chip] * 2,
        out_specs=[on_chip] * row_count,
        compiler_params=params(8),
        name="combine",
    )(kept, come)
    sums = [exchanged(sent[by - 1], "row", by) for by in range(1, row_count)]

    early, columns = pl.pallas_call(
        functools.partial(lookup_kernel, window),
        out_shape=[
            array(window * size, jnp.float32),
            jax.ShapeDtypeStruct((window * size, 1), jnp.int32),
        ],
        in_specs=[scalars] + [on_chip] * 4,
        out_specs=[on_chip] * 2,
        compiler_params=params(16 + 2 * window),
        cost_estimate=cost(window * size * 3 * owned * width),
        name="lookup",
    )(place, ids, item_table, near, following)
    far, early = lax.optimization_barrier((far, early))
    far2 = exchanged(far, "phase", 1)
    states = pl.pallas_call(
        functools.partial(section_kernel, window),
        out_shape=array(size),
        in_specs=[scalars] * 2 + [on_chip] * 4 + [anywhere] * 4 + [on_chip],
        out_specs=on_chip,
        scratch_shapes=[
            pltpu.VMEM((2,) + proj_weight.shape[1:], jnp.bfloat16),
            pltpu.VMEM((2,) + out_weight.shape[1:], jnp.bfloat16),
            pltpu.VMEM((window * size, width), jnp.float32),
            pltpu.VMEM((window * size, 4 * INNER), jnp.bfloat16),
            pltpu.VMEM((window * size, width), jnp.bfloat16),
            pltpu.VMEM((window * size, INNER), jnp.float32),
            pltpu.SemaphoreType.DMA((4,)),
        ],
        compiler_params=params(12 + 4 * window),
        cost_estimate=cost(8 * window * size * width * 2 * INNER),
        name="sections",
    )(
        place,
        seq_lengths,
        columns,
        early,
        far,
        far2,
        proj_weight,
        proj_other,
        out_weight,
        outw_other,
        final_gain.reshape(1, width),
    )
    own, states = lax.optimization_barrier((own, states))
    table_grad = pl.pallas_call(
        finish_kernel,
        out_shape=array(block, jnp.float32),
        in_specs=[on_chip] * row_count,
        out_specs=on_chip,
        compiler_params=params(8),
        name="finish",
    )(own, *sums)
    return (states.reshape(1, 1, size, width), table_grad)


def solution(mesh):
    placed = (
        P("emb", None),
        P("emb", "phase", "row", None),
        P("emb", "phase", "row"),
        P("emb", None, None),
        P("emb", "phase", "row", None),
        P("phase", None, None),
        P("phase", None, None),
        P(),
    )
    return jax.shard_map(
        body,
        mesh=mesh,
        in_specs=placed,
        out_specs=(P("emb", "phase", "row", None), P(("emb", "row", "phase"), None)),
        check_vma=False,
    )
```

```python
import functools

import jax
import jax.numpy as jnp
from jax import lax
from jax.experimental import pallas as pl
from jax.experimental.pallas import tpu as pltpu
from jax.sharding import PartitionSpec as P

HEADS = 4
HEAD_DIM = 128
INNER = HEADS * HEAD_DIM
SLOT_BASE = 128
CODE_ROWS = 16

norm_eps = 1e-05

NT = (((1,), (1,)), ((), ()))


def exchanged(shard, axis, by):
    count = lax.axis_size(axis)
    return lax.ppermute(shard, axis, [(i, i ^ by) for i in range(count)])


def layer_norm(values, times=1.0):
    average = jnp.mean(values, axis=-1, keepdims=True)
    centered = values - average
    variance = jnp.mean(centered * centered, axis=-1, keepdims=True)
    return centered * (times * lax.rsqrt(variance + norm_eps))


def silu_of_half(half):
    return half * jnp.tanh(half) + half


def dot(left, right):
    return jnp.dot(left, right, preferred_element_type=jnp.float32)


def as_column(row):
    count = row.shape[1]
    down = lax.broadcasted_iota(jnp.int32, (count, count), 0)
    along = lax.broadcasted_iota(jnp.int32, (count, count), 1)
    picked = jnp.where(down == along, jnp.broadcast_to(row, (count, count)), 0.0)
    return jnp.sum(picked, axis=1, keepdims=True)


def coded(numbers):
    high = numbers // SLOT_BASE
    low = numbers - high * SLOT_BASE
    line = lax.broadcasted_iota(jnp.int32, (CODE_ROWS, numbers.shape[1]), 0)
    codes = jnp.where(line == 0, high, jnp.where(line == 1, low, 0)).astype(jnp.float32)
    return codes.astype(jnp.bfloat16)


def decoded(codes):
    codes = codes.astype(jnp.float32)
    return codes[0:1] * SLOT_BASE + codes[1:2]


def pack_kernel(parties, capacity, owned, owner_ref, slot_ref, grad_ref, *packed_refs):
    my_phase = lax.axis_index("phase")
    owner = owner_ref[...] ^ lax.axis_index("emb")
    slot = slot_ref[...]
    count = owner.shape[1]
    width = grad_ref.shape[1]
    swapped = (owner // 2) | ((owner % 2) * 2)
    turned = jnp.where(my_phase == 0, owner, swapped)
    moved = slot + my_phase * (owned // 2)
    moved = jnp.where(moved >= owned, moved - owned, moved)
    packed_refs[parties][...] = turned * owned + jnp.where(turned > 0, moved, slot)
    before = (
        lax.broadcasted_iota(jnp.int32, (count, count), 0)
        < lax.broadcasted_iota(jnp.int32, (count, count), 1)
    ).astype(jnp.bfloat16)
    codes = coded(slot + SLOT_BASE)
    place = lax.broadcasted_iota(jnp.int32, (capacity, count), 0)
    chosen = []
    for party in range(parties):
        named = owner == party
        flags = jnp.broadcast_to(named, (CODE_ROWS, count)).astype(jnp.float32)
        rank = dot(flags.astype(jnp.bfloat16), before)[0:1].astype(jnp.int32)
        picks = (named & (rank == place)).astype(jnp.float32).astype(jnp.bfloat16)
        chosen.append(picks)
        sent = lax.dot_general(codes, picks, NT, preferred_element_type=jnp.float32)
        packed_refs[party][capacity : capacity + CODE_ROWS, :] = jnp.concatenate(
            [sent, jnp.zeros((CODE_ROWS, width - capacity), jnp.float32)], axis=1
        ).astype(jnp.bfloat16)
    for party in range(parties):
        rows = dot(chosen[party], grad_ref[...])
        packed_refs[party][0:capacity, :] = rows.astype(jnp.bfloat16)


def scatter_kernel(parties, capacity, row_ids, *refs):
    arrived = refs[:parties]
    keep_ref, send_ref = refs[parties:]
    rows, phases = row_ids
    my_row, my_phase = lax.axis_index("row"), lax.axis_index("phase")
    block = keep_ref.shape[0] // rows
    values = jnp.concatenate([ref[0:capacity, :] for ref in arrived], axis=0)
    slots = [
        decoded(ref[capacity : capacity + CODE_ROWS, 0:capacity]) - SLOT_BASE for ref in arrived
    ]
    slots = jnp.concatenate(slots, axis=1).astype(jnp.int32)
    down = lax.broadcasted_iota(jnp.int32, (block, parties * capacity), 0)
    for other in range(phases):
        for step in range(rows):
            base = ((my_row ^ step) * phases + (my_phase ^ other)) * block
            chosen = (slots - base == down).astype(jnp.float32).astype(jnp.bfloat16)
            total = dot(chosen, values)
            if other == 0:
                keep_ref[step * block : (step + 1) * block, :] = total
            else:
                send_ref[step * block : (step + 1) * block, :] = total.astype(jnp.bfloat16)


def combine_kernel(block, kept_ref, come_ref, own_ref, *sent_refs):
    for step in range(len(sent_refs) + 1):
        part = slice(step * block, (step + 1) * block)
        total = kept_ref[part, :] + come_ref[part, :].astype(jnp.float32)
        if step == 0:
            own_ref[...] = total
        else:
            sent_refs[step - 1][...] = total.astype(jnp.bfloat16)


def finish_kernel(own_ref, *refs):
    total = own_ref[...]
    for come_ref in refs[:-2]:
        total = total + come_ref[...].astype(jnp.float32)
    refs[-1][...] = total


def loop(count, body):
    if count <= 4:
        for index in range(count):
            body(index)
    else:
        lax.fori_loop(0, count, lambda index, carry: (body(index), carry)[1], 0)


def rows_at(start, count, step):
    if isinstance(start, int):
        return pl.ds(start, count)
    return pl.ds(pl.multiple_of(start, step), count)


def tall_blocks(window):
    return window if window <= 4 else 1


def look_up(ids, pieces):
    total = None
    for base, piece in pieces:
        along = lax.broadcasted_iota(jnp.int32, (ids.shape[0], piece.shape[0]), 1)
        chosen = (along == ids - base).astype(jnp.float32).astype(jnp.bfloat16)
        part = dot(chosen, piece[...])
        total = part if total is None else total + part
    return total


def half_kernel(table_ref, half_ref):
    half = half_ref.shape[0]
    start = pl.multiple_of(lax.axis_index("phase") * half, half)
    half_ref[...] = table_ref[pl.ds(start, half), :]


def join_kernel(first_ref, second_ref, joined_ref):
    count = first_ref.shape[0]
    joined_ref[0:count, :] = first_ref[...]
    joined_ref[count:, :] = second_ref[...]


def lookup_kernel(
    window,
    ids_ref,
    lengths_ref,
    table_ref,
    near_ref,
    next_ref,
    near2_ref,
    next2_ref,
    emb_ref,
    column_ref,
    earliest_ref,
):
    my_row = lax.axis_index("row")
    my_phase = lax.axis_index("phase")
    size = ids_ref.shape[1]
    owned, half = table_ref.shape[0], near_ref.shape[0]

    def column(index):
        row = my_row - (window - 1) + index
        ids = ids_ref[pl.ds(jnp.maximum(row, 0) ^ my_row, 1), :].astype(jnp.float32)
        return as_column(jnp.where(row >= 0, ids, -1.0))

    tall = tall_blocks(window)
    height = tall * size
    pieces = (
        (0, table_ref),
        (owned, near_ref),
        (owned + half, next2_ref),
        (2 * owned, next_ref),
        (2 * owned + half, near2_ref),
    )

    def step(index):
        part = rows_at(index * height, height, size)
        ids = [column(index * tall + block) for block in range(tall)]
        ids = jnp.concatenate(ids, axis=0).astype(jnp.int32)
        emb_ref[part, :] = look_up(ids, pieces).astype(jnp.bfloat16)
        column_ref[part, :] = ids - 3 * owned
        position = (my_row - (window - 1)) * size + index * height
        position = position + lax.broadcasted_iota(jnp.int32, (height, 1), 0)
        earliest = jnp.zeros((height, 1), jnp.int32)
        bound = jnp.int32(0)
        for segment in range(lengths_ref.shape[2] - 1):
            bound = bound + lengths_ref[0, my_phase, segment]
            earliest = jnp.where(position >= bound, bound, earliest)
        earliest_ref[part, :] = earliest

    loop(window // tall, step)


def weights_kernel(proj_own, proj_other, outw_own, outw_other, proj_ref, outw_ref, sems):
    my_phase = lax.axis_index("phase")
    copies = [
        pltpu.make_async_copy(proj_own.at[0], proj_ref.at[my_phase], sems.at[0]),
        pltpu.make_async_copy(proj_other.at[0], proj_ref.at[1 - my_phase], sems.at[1]),
        pltpu.make_async_copy(outw_own.at[0], outw_ref.at[my_phase], sems.at[2]),
        pltpu.make_async_copy(outw_other.at[0], outw_ref.at[1 - my_phase], sems.at[3]),
    ]
    for copy in copies:
        copy.start()
    for copy in copies:
        copy.wait()


def section_kernel(
    window,
    earliest_ref,
    ids_ref,
    early_ref,
    far_ref,
    far2_ref,
    proj_ref,
    outw_ref,
    gain_ref,
    out_ref,
    done_ref,
    emb_ref,
    act_ref,
    mid_ref,
    mix_ref,
):
    my_row = lax.axis_index("row")
    size = out_ref.shape[0]
    half = far_ref.shape[0]
    tall = tall_blocks(window)
    height = tall * size

    def rows(start, count=height):
        return rows_at(start, count, size)

    def late(step):
        part = rows(step * height)
        found = look_up(ids_ref[part, :], ((0, far_ref), (half, far2_ref)))
        emb_ref[part, :] = early_ref[part, :].astype(jnp.float32) + found

    loop(window // tall, late)

    first_pos = (my_row - (window - 1)) * size
    across = lax.broadcasted_iota(jnp.int32, (1, size), 1)

    def attend(start, count, key_start, diagonal):
        query_pos = first_pos + start + lax.broadcasted_iota(jnp.int32, (count, 1), 0)
        key_pos = first_pos + key_start + across
        visible = key_pos >= earliest_ref[rows(start, count), :]
        if diagonal:
            visible = visible & (key_pos <= query_pos)
        for head in range(HEADS):
            cols = head * HEAD_DIM
            queries = act_ref[rows(start, count), 2 * INNER + cols : 2 * INNER + cols + HEAD_DIM]
            keys = act_ref[rows(key_start, size), 3 * INNER + cols : 3 * INNER + cols + HEAD_DIM]
            values = act_ref[rows(key_start, size), INNER + cols : INNER + cols + HEAD_DIM]
            scores = lax.dot_general(queries, keys, NT, preferred_element_type=jnp.float32)
            weights = jnp.where(visible, silu_of_half(scores), 0.0).astype(jnp.bfloat16)
            mix_ref[rows(start, count), cols : cols + HEAD_DIM] += dot(weights, values)

    def project(start, count, section, parts):
        source = emb_ref if section == 0 else mid_ref
        values = source[rows(start, count), :].astype(jnp.float32)
        normed = layer_norm(values, 0.5).astype(jnp.bfloat16)
        for part in parts:
            cols = part * INNER
            act = silu_of_half(dot(normed, proj_ref[section, :, cols : cols + INNER]))
            if part == 2:
                act = 0.5 * act
            act_ref[rows(start, count), cols : cols + INNER] = act.astype(jnp.bfloat16)

    def finish(start, count, section):
        source = emb_ref if section == 0 else mid_ref
        values = source[rows(start, count), :].astype(jnp.float32)
        gates = act_ref[rows(start, count), 0:INNER].astype(jnp.float32)
        gated = (layer_norm(mix_ref[rows(start, count), :]) * gates).astype(jnp.bfloat16)
        return values + dot(gated, outw_ref[section])

    last = (window - 1) * size
    mix_ref[...] = jnp.zeros(mix_ref.shape, jnp.float32)
    loop(window // tall, lambda step: project(step * height, height, 0, (3, 2, 1, 0)))
    if tall == window:
        for block in range(window):
            attend(block * size, height - block * size, block * size, True)
    else:

        def with_keys(block):
            attend(block * size, size, block * size, True)
            lax.fori_loop(
                block + 1,
                window,
                lambda later, c: (attend(later * size, size, block * size, False), c)[1],
                0,
            )

        loop(window, with_keys)

    def close_first(step):
        mid_ref[rows(step * height), :] = finish(step * height, height, 0).astype(jnp.bfloat16)

    loop(window // tall, close_first)
    mix_ref[last : last + size, :] = jnp.zeros((size, INNER), jnp.float32)
    loop(window // tall, lambda step: project(step * height, height, 1, (3, 1)))
    project(last, size, 1, (2, 0))
    attend(last, size, last, True)
    loop(window - 1, lambda block: attend(last, size, block * size, False))
    closing = finish(last, size, 1)
    out_ref[...] = (layer_norm(closing) * gain_ref[...]).astype(jnp.bfloat16)
    done_ref[...] = jnp.zeros(done_ref.shape, jnp.float32)


def body(
    item_table, item_owner, item_slot, seq_lengths, row_grads, proj_weight, out_weight, final_gain
):
    parties = lax.axis_size("emb")
    row_count = lax.axis_size("row")
    phases = lax.axis_size("phase")
    my_emb = lax.axis_index("emb")
    my_row = lax.axis_index("row")
    my_phase = lax.axis_index("phase")
    size = item_slot.shape[2]
    width = item_table.shape[1]
    owned = item_table.shape[0]
    half = owned // 2
    capacity = max(16, 2 * size // parties)
    window = -(-3 * row_count // 4)
    vmem = pltpu.MemorySpace.VMEM
    smem = pltpu.MemorySpace.SMEM

    def params(mebibytes):
        return pltpu.CompilerParams(vmem_limit_bytes=mebibytes * 1024 * 1024)

    def across(shard, first):
        pairs = []
        for emb in range(parties):
            for phase in range(phases):
                by = 1 if (phase == 0) == first else 2
                pairs.append((emb * phases + phase, (emb ^ by) * phases + phase))
        return lax.ppermute(shard, ("emb", "phase"), pairs)

    proj_other = exchanged(proj_weight, "phase", 1)
    outw_other = exchanged(out_weight, "phase", 1)

    on_chip = pl.BlockSpec(memory_space=vmem)
    scalars = pl.BlockSpec(memory_space=smem)
    anywhere = pl.BlockSpec(memory_space=pl.ANY)

    def array(rows, dtype=jnp.bfloat16):
        return jax.ShapeDtypeStruct((rows, width), dtype)

    owners, slots = item_owner.reshape(1, size), item_slot.reshape(1, size)
    *packed, ids = pl.pallas_call(
        functools.partial(pack_kernel, parties, capacity, owned),
        out_shape=[array(capacity + CODE_ROWS)] * parties
        + [jax.ShapeDtypeStruct((1, size), jnp.int32)],
        in_specs=[on_chip] * 3,
        out_specs=[on_chip] * (parties + 1),
        compiler_params=params(4),
        name="pack",
    )(owners, slots, row_grads.reshape(size, width))
    arrived = [packed[0]] + [exchanged(packed[by], "emb", by) for by in range(1, parties)]
    own_half = pl.pallas_call(
        half_kernel,
        out_shape=array(half),
        in_specs=[on_chip],
        out_specs=on_chip,
        compiler_params=params(4),
        name="half",
    )(item_table)
    near = across(own_half, True)
    following = across(own_half, False)
    far = across(near, False)
    near2 = exchanged(near, "phase", 1)
    next2 = exchanged(following, "phase", 1)
    by = 1
    while by < row_count:
        ids = pl.pallas_call(
            join_kernel,
            out_shape=jax.ShapeDtypeStruct((2 * by, size), jnp.int32),
            in_specs=[on_chip] * 2,
            out_specs=on_chip,
            compiler_params=params(4),
            name="join",
        )(ids, exchanged(ids, "row", by))
        by *= 2
    ids, *arrived = lax.optimization_barrier((ids, *arrived))
    block = owned // (row_count * phases)
    count = row_count * block
    kept, sent = pl.pallas_call(
        functools.partial(scatter_kernel, parties, capacity, (row_count, phases)),
        out_shape=[array(count, jnp.float32), array(count)],
        in_specs=[on_chip] * parties,
        out_specs=[on_chip] * 2,
        compiler_params=params(4),
        cost_estimate=pl.CostEstimate(flops=32999999999, bytes_accessed=0, transcendentals=0),
        name="scatter",
    )(*arrived)
    come = exchanged(sent, "phase", 1)
    own, *sent = pl.pallas_call(
        functools.partial(combine_kernel, block),
        out_shape=[array(block, jnp.float32)] + [array(block)] * (row_count - 1),
        in_specs=[on_chip] * 2,
        out_specs=[on_chip] * row_count,
        compiler_params=params(4),
        name="combine",
    )(kept, come)
    sums = [exchanged(sent[by - 1], "row", by) for by in range(1, row_count)]

    early, columns, earliest = pl.pallas_call(
        functools.partial(lookup_kernel, window),
        out_shape=[
            array(window * size),
            jax.ShapeDtypeStruct((window * size, 1), jnp.int32),
            jax.ShapeDtypeStruct((window * size, 1), jnp.int32),
        ],
        in_specs=[on_chip, scalars] + [on_chip] * 5,
        out_specs=[on_chip] * 3,
        compiler_params=params(8 + window),
        name="lookup",
    )(ids, seq_lengths, item_table, near, following, near2, next2)
    proj_both, outw_both = pl.pallas_call(
        weights_kernel,
        out_shape=[
            jax.ShapeDtypeStruct((2,) + proj_weight.shape[1:], jnp.bfloat16),
            jax.ShapeDtypeStruct((2,) + out_weight.shape[1:], jnp.bfloat16),
        ],
        in_specs=[anywhere] * 4,
        out_specs=[on_chip] * 2,
        scratch_shapes=[pltpu.SemaphoreType.DMA((4,))],
        compiler_params=params(8),
        name="weights",
    )(proj_weight, proj_other, out_weight, outw_other)
    far, early, outw_both = lax.optimization_barrier((far, early, outw_both))
    far2 = exchanged(far, "phase", 1)
    states, done = pl.pallas_call(
        functools.partial(section_kernel, window),
        out_shape=[array(size), jax.ShapeDtypeStruct((8, 128), jnp.float32)],
        in_specs=[on_chip] * 8,
        out_specs=[on_chip] * 2,
        scratch_shapes=[
            pltpu.VMEM((window * size, width), jnp.float32),
            pltpu.VMEM((window * size, 4 * INNER), jnp.bfloat16),
            pltpu.VMEM((window * size, width), jnp.bfloat16),
            pltpu.VMEM((window * size, INNER), jnp.float32),
        ],
        compiler_params=params(10 + 4 * window),
        cost_estimate=pl.CostEstimate(flops=1, bytes_accessed=1, transcendentals=0),
        name="sections",
    )(
        earliest,
        columns,
        early,
        far,
        far2,
        proj_both,
        outw_both,
        final_gain.reshape(1, width),
    )
    table_grad = pl.pallas_call(
        finish_kernel,
        out_shape=array(block, jnp.float32),
        in_specs=[on_chip] * row_count + [anywhere],
        out_specs=on_chip,
        compiler_params=params(4),
        name="finish",
    )(own, *sums, done)
    return (states.reshape(1, 1, size, width), table_grad)


def solution(mesh):
    placed = (
        P("emb", None),
        P("emb", "phase", "row", None),
        P("emb", "phase", "row"),
        P("emb", None, None),
        P("emb", "phase", "row", None),
        P("phase", None, None),
        P("phase", None, None),
        P(),
    )
    return jax.shard_map(
        body,
        mesh=mesh,
        in_specs=placed,
        out_specs=(P("emb", "phase", "row", None), P(("emb", "row", "phase"), None)),
        check_vma=False,
    )
```

```python
import functools

import jax
import jax.numpy as jnp
from jax import lax
from jax.experimental import pallas as pl
from jax.experimental.pallas import tpu as pltpu
from jax.sharding import PartitionSpec as P

HEADS = 4
HEAD_DIM = 128
INNER = HEADS * HEAD_DIM
SLOT_BASE = 128
CODE_ROWS = 16

norm_eps = 1e-05

NT = (((1,), (1,)), ((), ()))


def exchanged(shard, axis, by):
    count = lax.axis_size(axis)
    return lax.ppermute(shard, axis, [(i, i ^ by) for i in range(count)])


def layer_norm(values, times=1.0):
    average = jnp.mean(values, axis=-1, keepdims=True)
    centered = values - average
    variance = jnp.mean(centered * centered, axis=-1, keepdims=True)
    return centered * (times * lax.rsqrt(variance + norm_eps))


def silu_of_half(half):
    return half * jnp.tanh(half) + half


def dot(left, right):
    return jnp.dot(left, right, preferred_element_type=jnp.float32)


def as_column(row):
    count = row.shape[1]
    down = lax.broadcasted_iota(jnp.int32, (count, count), 0)
    along = lax.broadcasted_iota(jnp.int32, (count, count), 1)
    picked = jnp.where(down == along, jnp.broadcast_to(row, (count, count)), 0.0)
    return jnp.sum(picked, axis=1, keepdims=True)


def coded(numbers):
    high = numbers // SLOT_BASE
    low = numbers - high * SLOT_BASE
    line = lax.broadcasted_iota(jnp.int32, (CODE_ROWS, numbers.shape[1]), 0)
    codes = jnp.where(line == 0, high, jnp.where(line == 1, low, 0)).astype(jnp.float32)
    return codes.astype(jnp.bfloat16)


def decoded(codes):
    codes = codes.astype(jnp.float32)
    return codes[0:1] * SLOT_BASE + codes[1:2]


def pack_kernel(parties, capacity, owned, owner_ref, slot_ref, grad_ref, *packed_refs):
    my_phase = lax.axis_index("phase")
    owner = owner_ref[...] ^ lax.axis_index("emb")
    slot = slot_ref[...]
    count = owner.shape[1]
    width = grad_ref.shape[1]
    swapped = (owner // 2) | ((owner % 2) * 2)
    turned = jnp.where(my_phase == 0, owner, swapped)
    moved = slot + my_phase * (owned // 2)
    moved = jnp.where(moved >= owned, moved - owned, moved)
    packed_refs[parties][...] = turned * owned + jnp.where(turned == 3, moved, slot)
    before = (
        lax.broadcasted_iota(jnp.int32, (count, count), 0)
        < lax.broadcasted_iota(jnp.int32, (count, count), 1)
    ).astype(jnp.bfloat16)
    codes = coded(slot + SLOT_BASE)
    place = lax.broadcasted_iota(jnp.int32, (capacity, count), 0)
    chosen = []
    for party in range(parties):
        named = owner == party
        flags = jnp.broadcast_to(named, (CODE_ROWS, count)).astype(jnp.float32)
        rank = dot(flags.astype(jnp.bfloat16), before)[0:1].astype(jnp.int32)
        picks = (named & (rank == place)).astype(jnp.float32).astype(jnp.bfloat16)
        chosen.append(picks)
        sent = lax.dot_general(codes, picks, NT, preferred_element_type=jnp.float32)
        packed_refs[party][capacity : capacity + CODE_ROWS, :] = jnp.concatenate(
            [sent, jnp.zeros((CODE_ROWS, width - capacity), jnp.float32)], axis=1
        ).astype(jnp.bfloat16)
    for party in range(parties):
        rows = dot(chosen[party], grad_ref[...])
        packed_refs[party][0:capacity, :] = rows.astype(jnp.bfloat16)


def scatter_kernel(parties, capacity, row_ids, *refs):
    arrived = refs[:parties]
    keep_ref, send_ref = refs[parties:]
    rows, phases = row_ids
    my_row, my_phase = lax.axis_index("row"), lax.axis_index("phase")
    block = keep_ref.shape[0] // rows
    values = jnp.concatenate([ref[0:capacity, :] for ref in arrived], axis=0)
    slots = [
        decoded(ref[capacity : capacity + CODE_ROWS, 0:capacity]) - SLOT_BASE for ref in arrived
    ]
    slots = jnp.concatenate(slots, axis=1).astype(jnp.int32)
    down = lax.broadcasted_iota(jnp.int32, (block, parties * capacity), 0)
    for other in range(phases):
        for step in range(rows):
            base = ((my_row ^ step) * phases + (my_phase ^ other)) * block
            chosen = (slots - base == down).astype(jnp.float32).astype(jnp.bfloat16)
            total = dot(chosen, values)
            if other == 0:
                keep_ref[step * block : (step + 1) * block, :] = total
            else:
                send_ref[step * block : (step + 1) * block, :] = total.astype(jnp.bfloat16)


def combine_kernel(block, kept_ref, come_ref, own_ref, *sent_refs):
    for step in range(len(sent_refs) + 1):
        part = slice(step * block, (step + 1) * block)
        total = kept_ref[part, :] + come_ref[part, :].astype(jnp.float32)
        if step == 0:
            own_ref[...] = total
        else:
            sent_refs[step - 1][...] = total.astype(jnp.bfloat16)


def finish_kernel(own_ref, *refs):
    total = own_ref[...]
    for come_ref in refs[:-2]:
        total = total + come_ref[...].astype(jnp.float32)
    refs[-1][...] = total


def loop(count, body):
    if count <= 4:
        for index in range(count):
            body(index)
    else:
        lax.fori_loop(0, count, lambda index, carry: (body(index), carry)[1], 0)


def rows_at(start, count, step):
    if isinstance(start, int):
        return pl.ds(start, count)
    return pl.ds(pl.multiple_of(start, step), count)


def tall_blocks(window):
    return window if window <= 4 else 1


def look_up(ids, pieces):
    total = None
    for base, piece in pieces:
        along = lax.broadcasted_iota(jnp.int32, (ids.shape[0], piece.shape[0]), 1)
        chosen = (along == ids - base).astype(jnp.float32).astype(jnp.bfloat16)
        part = dot(chosen, piece[...])
        total = part if total is None else total + part
    return total


def half_kernel(table_ref, half_ref):
    half = half_ref.shape[0]
    start = pl.multiple_of(lax.axis_index("phase") * half, half)
    half_ref[...] = table_ref[pl.ds(start, half), :]


def join_kernel(first_ref, second_ref, joined_ref):
    count = first_ref.shape[0]
    joined_ref[0:count, :] = first_ref[...]
    joined_ref[count:, :] = second_ref[...]


def lookup_kernel(
    window,
    ids_ref,
    lengths_ref,
    table_ref,
    near_ref,
    next_ref,
    emb_ref,
    column_ref,
    earliest_ref,
):
    my_row = lax.axis_index("row")
    my_phase = lax.axis_index("phase")
    size = ids_ref.shape[1]
    owned = table_ref.shape[0]

    def column(index):
        row = my_row - (window - 1) + index
        ids = ids_ref[pl.ds(jnp.maximum(row, 0) ^ my_row, 1), :].astype(jnp.float32)
        return as_column(jnp.where(row >= 0, ids, -1.0))

    tall = tall_blocks(window)
    height = tall * size
    pieces = ((0, table_ref), (owned, near_ref), (2 * owned, next_ref))

    def step(index):
        part = rows_at(index * height, height, size)
        ids = [column(index * tall + block) for block in range(tall)]
        ids = jnp.concatenate(ids, axis=0).astype(jnp.int32)
        emb_ref[part, :] = look_up(ids, pieces).astype(jnp.bfloat16)
        column_ref[part, :] = ids - 3 * owned
        position = (my_row - (window - 1)) * size + index * height
        position = position + lax.broadcasted_iota(jnp.int32, (height, 1), 0)
        earliest = jnp.zeros((height, 1), jnp.int32)
        bound = jnp.int32(0)
        for segment in range(lengths_ref.shape[2] - 1):
            bound = bound + lengths_ref[0, my_phase, segment]
            earliest = jnp.where(position >= bound, bound, earliest)
        earliest_ref[part, :] = earliest

    loop(window // tall, step)


def weights_kernel(proj_own, proj_other, outw_own, outw_other, proj_ref, outw_ref, sems):
    my_phase = lax.axis_index("phase")
    copies = [
        pltpu.make_async_copy(proj_own.at[0], proj_ref.at[my_phase], sems.at[0]),
        pltpu.make_async_copy(proj_other.at[0], proj_ref.at[1 - my_phase], sems.at[1]),
        pltpu.make_async_copy(outw_own.at[0], outw_ref.at[my_phase], sems.at[2]),
        pltpu.make_async_copy(outw_other.at[0], outw_ref.at[1 - my_phase], sems.at[3]),
    ]
    for copy in copies:
        copy.start()
    for copy in copies:
        copy.wait()


def section_kernel(
    window,
    earliest_ref,
    ids_ref,
    early_ref,
    far_ref,
    far2_ref,
    proj_ref,
    outw_ref,
    gain_ref,
    out_ref,
    done_ref,
    emb_ref,
    act_ref,
    mid_ref,
    mix_ref,
):
    my_row = lax.axis_index("row")
    size = out_ref.shape[0]
    half = far_ref.shape[0]
    tall = tall_blocks(window)
    height = tall * size

    def rows(start, count=height):
        return rows_at(start, count, size)

    def late(step):
        part = rows(step * height)
        found = look_up(ids_ref[part, :], ((0, far_ref), (half, far2_ref)))
        emb_ref[part, :] = early_ref[part, :].astype(jnp.float32) + found

    loop(window // tall, late)

    first_pos = (my_row - (window - 1)) * size
    across = lax.broadcasted_iota(jnp.int32, (1, size), 1)

    def attend(start, count, key_start, diagonal):
        query_pos = first_pos + start + lax.broadcasted_iota(jnp.int32, (count, 1), 0)
        key_pos = first_pos + key_start + across
        visible = key_pos >= earliest_ref[rows(start, count), :]
        if diagonal:
            visible = visible & (key_pos <= query_pos)
        for head in range(HEADS):
            cols = head * HEAD_DIM
            queries = act_ref[rows(start, count), 2 * INNER + cols : 2 * INNER + cols + HEAD_DIM]
            keys = act_ref[rows(key_start, size), 3 * INNER + cols : 3 * INNER + cols + HEAD_DIM]
            values = act_ref[rows(key_start, size), INNER + cols : INNER + cols + HEAD_DIM]
            scores = lax.dot_general(queries, keys, NT, preferred_element_type=jnp.float32)
            weights = jnp.where(visible, silu_of_half(scores), 0.0).astype(jnp.bfloat16)
            mix_ref[rows(start, count), cols : cols + HEAD_DIM] += dot(weights, values)

    def project(start, count, section, parts):
        source = emb_ref if section == 0 else mid_ref
        values = source[rows(start, count), :].astype(jnp.float32)
        normed = layer_norm(values, 0.5).astype(jnp.bfloat16)
        for part in parts:
            cols = part * INNER
            act = silu_of_half(dot(normed, proj_ref[section, :, cols : cols + INNER]))
            if part == 2:
                act = 0.5 * act
            act_ref[rows(start, count), cols : cols + INNER] = act.astype(jnp.bfloat16)

    def finish(start, count, section):
        source = emb_ref if section == 0 else mid_ref
        values = source[rows(start, count), :].astype(jnp.float32)
        gates = act_ref[rows(start, count), 0:INNER].astype(jnp.float32)
        gated = (layer_norm(mix_ref[rows(start, count), :]) * gates).astype(jnp.bfloat16)
        return values + dot(gated, outw_ref[section])

    last = (window - 1) * size
    mix_ref[...] = jnp.zeros(mix_ref.shape, jnp.float32)
    loop(window // tall, lambda step: project(step * height, height, 0, (3, 2, 1, 0)))
    if tall == window:
        for block in range(window):
            attend(block * size, height - block * size, block * size, True)
    else:

        def with_keys(block):
            attend(block * size, size, block * size, True)
            lax.fori_loop(
                block + 1,
                window,
                lambda later, c: (attend(later * size, size, block * size, False), c)[1],
                0,
            )

        loop(window, with_keys)

    def close_first(step):
        mid_ref[rows(step * height), :] = finish(step * height, height, 0).astype(jnp.bfloat16)

    loop(window // tall, close_first)
    mix_ref[last : last + size, :] = jnp.zeros((size, INNER), jnp.float32)
    loop(window // tall, lambda step: project(step * height, height, 1, (3, 1)))
    project(last, size, 1, (2, 0))
    attend(last, size, last, True)
    loop(window - 1, lambda block: attend(last, size, block * size, False))
    closing = finish(last, size, 1)
    out_ref[...] = (layer_norm(closing) * gain_ref[...]).astype(jnp.bfloat16)
    done_ref[...] = jnp.zeros(done_ref.shape, jnp.float32)


def body(
    item_table, item_owner, item_slot, seq_lengths, row_grads, proj_weight, out_weight, final_gain
):
    parties = lax.axis_size("emb")
    row_count = lax.axis_size("row")
    phases = lax.axis_size("phase")
    my_emb = lax.axis_index("emb")
    my_row = lax.axis_index("row")
    my_phase = lax.axis_index("phase")
    size = item_slot.shape[2]
    width = item_table.shape[1]
    owned = item_table.shape[0]
    half = owned // 2
    capacity = max(16, 2 * size // parties)
    window = -(-3 * row_count // 4)
    vmem = pltpu.MemorySpace.VMEM
    smem = pltpu.MemorySpace.SMEM

    def params(mebibytes):
        return pltpu.CompilerParams(vmem_limit_bytes=mebibytes * 1024 * 1024)

    def across(shard, first):
        pairs = []
        for emb in range(parties):
            for phase in range(phases):
                by = 1 if (phase == 0) == first else 2
                pairs.append((emb * phases + phase, (emb ^ by) * phases + phase))
        return lax.ppermute(shard, ("emb", "phase"), pairs)

    proj_other = exchanged(proj_weight, "phase", 1)
    outw_other = exchanged(out_weight, "phase", 1)

    on_chip = pl.BlockSpec(memory_space=vmem)
    scalars = pl.BlockSpec(memory_space=smem)
    anywhere = pl.BlockSpec(memory_space=pl.ANY)

    def array(rows, dtype=jnp.bfloat16):
        return jax.ShapeDtypeStruct((rows, width), dtype)

    owners, slots = item_owner.reshape(1, size), item_slot.reshape(1, size)
    *packed, ids = pl.pallas_call(
        functools.partial(pack_kernel, parties, capacity, owned),
        out_shape=[array(capacity + CODE_ROWS)] * parties
        + [jax.ShapeDtypeStruct((1, size), jnp.int32)],
        in_specs=[on_chip] * 3,
        out_specs=[on_chip] * (parties + 1),
        compiler_params=params(4),
        name="pack",
    )(owners, slots, row_grads.reshape(size, width))
    arrived = [packed[0]] + [exchanged(packed[by], "emb", by) for by in range(1, parties)]
    near = across(item_table, True)
    by = 1
    while by < row_count:
        ids = pl.pallas_call(
            join_kernel,
            out_shape=jax.ShapeDtypeStruct((2 * by, size), jnp.int32),
            in_specs=[on_chip] * 2,
            out_specs=on_chip,
            compiler_params=params(4),
            name="join",
        )(ids, exchanged(ids, "row", by))
        by *= 2
    near, ids = lax.optimization_barrier((near, ids))
    following = exchanged(near, "phase", 1)
    near_half = pl.pallas_call(
        half_kernel,
        out_shape=array(half),
        in_specs=[on_chip],
        out_specs=on_chip,
        compiler_params=params(4),
        name="half",
    )(near)
    far = across(near_half, False)
    ids, *arrived = lax.optimization_barrier((ids, *arrived))
    block = owned // (row_count * phases)
    count = row_count * block
    kept, sent = pl.pallas_call(
        functools.partial(scatter_kernel, parties, capacity, (row_count, phases)),
        out_shape=[array(count, jnp.float32), array(count)],
        in_specs=[on_chip] * parties,
        out_specs=[on_chip] * 2,
        compiler_params=params(4),
        cost_estimate=pl.CostEstimate(flops=32999999999, bytes_accessed=0, transcendentals=0),
        name="scatter",
    )(*arrived)
    come = exchanged(sent, "phase", 1)
    own, *sent = pl.pallas_call(
        functools.partial(combine_kernel, block),
        out_shape=[array(block, jnp.float32)] + [array(block)] * (row_count - 1),
        in_specs=[on_chip] * 2,
        out_specs=[on_chip] * row_count,
        compiler_params=params(4),
        name="combine",
    )(kept, come)
    sums = [exchanged(sent[by - 1], "row", by) for by in range(1, row_count)]

    early, columns, earliest = pl.pallas_call(
        functools.partial(lookup_kernel, window),
        out_shape=[
            array(window * size),
            jax.ShapeDtypeStruct((window * size, 1), jnp.int32),
            jax.ShapeDtypeStruct((window * size, 1), jnp.int32),
        ],
        in_specs=[on_chip, scalars] + [on_chip] * 3,
        out_specs=[on_chip] * 3,
        compiler_params=params(8 + window),
        name="lookup",
    )(ids, seq_lengths, item_table, near, following)
    proj_both, outw_both = pl.pallas_call(
        weights_kernel,
        out_shape=[
            jax.ShapeDtypeStruct((2,) + proj_weight.shape[1:], jnp.bfloat16),
            jax.ShapeDtypeStruct((2,) + out_weight.shape[1:], jnp.bfloat16),
        ],
        in_specs=[anywhere] * 4,
        out_specs=[on_chip] * 2,
        scratch_shapes=[pltpu.SemaphoreType.DMA((4,))],
        compiler_params=params(8),
        name="weights",
    )(proj_weight, proj_other, out_weight, outw_other)
    far, early, outw_both = lax.optimization_barrier((far, early, outw_both))
    far2 = exchanged(far, "phase", 1)
    states, done = pl.pallas_call(
        functools.partial(section_kernel, window),
        out_shape=[array(size), jax.ShapeDtypeStruct((8, 128), jnp.float32)],
        in_specs=[on_chip] * 8,
        out_specs=[on_chip] * 2,
        scratch_shapes=[
            pltpu.VMEM((window * size, width), jnp.float32),
            pltpu.VMEM((window * size, 4 * INNER), jnp.bfloat16),
            pltpu.VMEM((window * size, width), jnp.bfloat16),
            pltpu.VMEM((window * size, INNER), jnp.float32),
        ],
        compiler_params=params(10 + 4 * window),
        cost_estimate=pl.CostEstimate(flops=1, bytes_accessed=1, transcendentals=0),
        name="sections",
    )(
        earliest,
        columns,
        early,
        far,
        far2,
        proj_both,
        outw_both,
        final_gain.reshape(1, width),
    )
    table_grad = pl.pallas_call(
        finish_kernel,
        out_shape=array(block, jnp.float32),
        in_specs=[on_chip] * row_count + [anywhere],
        out_specs=on_chip,
        compiler_params=params(4),
        name="finish",
    )(own, *sums, done)
    return (states.reshape(1, 1, size, width), table_grad)


def solution(mesh):
    placed = (
        P("emb", None),
        P("emb", "phase", "row", None),
        P("emb", "phase", "row"),
        P("emb", None, None),
        P("emb", "phase", "row", None),
        P("phase", None, None),
        P("phase", None, None),
        P(),
    )
    return jax.shard_map(
        body,
        mesh=mesh,
        in_specs=placed,
        out_specs=(P("emb", "phase", "row", None), P(("emb", "row", "phase"), None)),
        check_vma=False,
    )
```

```python
import functools

import jax
import jax.numpy as jnp
from jax import lax
from jax.experimental import pallas as pl
from jax.experimental.pallas import tpu as pltpu
from jax.sharding import PartitionSpec as P

HEADS = 4
HEAD_DIM = 128
INNER = HEADS * HEAD_DIM
SLOT_BASE = 128
CODE_ROWS = 16

norm_eps = 1e-05

NT = (((1,), (1,)), ((), ()))


def exchanged(shard, axis, by):
    count = lax.axis_size(axis)
    return lax.ppermute(shard, axis, [(i, i ^ by) for i in range(count)])


def layer_norm(values, times=1.0):
    average = jnp.mean(values, axis=-1, keepdims=True)
    centered = values - average
    variance = jnp.mean(centered * centered, axis=-1, keepdims=True)
    return centered * (times * lax.rsqrt(variance + norm_eps))


def silu_of_half(half):
    return half * jnp.tanh(half) + half


def dot(left, right):
    return jnp.dot(left, right, preferred_element_type=jnp.float32)


def as_column(row):
    count = row.shape[1]
    down = lax.broadcasted_iota(jnp.int32, (count, count), 0)
    along = lax.broadcasted_iota(jnp.int32, (count, count), 1)
    picked = jnp.where(down == along, jnp.broadcast_to(row, (count, count)), 0.0)
    return jnp.sum(picked, axis=1, keepdims=True)


def coded(numbers):
    high = numbers // SLOT_BASE
    low = numbers - high * SLOT_BASE
    line = lax.broadcasted_iota(jnp.int32, (CODE_ROWS, numbers.shape[1]), 0)
    codes = jnp.where(line == 0, high, jnp.where(line == 1, low, 0)).astype(jnp.float32)
    return codes.astype(jnp.bfloat16)


def decoded(codes):
    codes = codes.astype(jnp.float32)
    return codes[0:1] * SLOT_BASE + codes[1:2]


def pack_kernel(parties, capacity, owned, owner_ref, slot_ref, grad_ref, *packed_refs):
    my_phase = lax.axis_index("phase")
    owner = owner_ref[...] ^ lax.axis_index("emb")
    slot = slot_ref[...]
    count = owner.shape[1]
    width = grad_ref.shape[1]
    swapped = (owner // 2) | ((owner % 2) * 2)
    turned = jnp.where(my_phase == 0, owner, swapped)
    moved = slot + my_phase * (owned // 2)
    moved = jnp.where(moved >= owned, moved - owned, moved)
    packed_refs[parties][...] = turned * owned + jnp.where(turned == 3, moved, slot)
    before = (
        lax.broadcasted_iota(jnp.int32, (count, count), 0)
        < lax.broadcasted_iota(jnp.int32, (count, count), 1)
    ).astype(jnp.bfloat16)
    codes = coded(slot + SLOT_BASE)
    place = lax.broadcasted_iota(jnp.int32, (capacity, count), 0)
    chosen = []
    for party in range(parties):
        named = owner == party
        flags = jnp.broadcast_to(named, (CODE_ROWS, count)).astype(jnp.float32)
        rank = dot(flags.astype(jnp.bfloat16), before)[0:1].astype(jnp.int32)
        picks = (named & (rank == place)).astype(jnp.float32).astype(jnp.bfloat16)
        chosen.append(picks)
        sent = lax.dot_general(codes, picks, NT, preferred_element_type=jnp.float32)
        packed_refs[party][capacity : capacity + CODE_ROWS, :] = jnp.concatenate(
            [sent, jnp.zeros((CODE_ROWS, width - capacity), jnp.float32)], axis=1
        ).astype(jnp.bfloat16)
    for party in range(parties):
        rows = dot(chosen[party], grad_ref[...])
        packed_refs[party][0:capacity, :] = rows.astype(jnp.bfloat16)


def scatter_kernel(parties, capacity, row_ids, *refs):
    arrived = refs[:parties]
    keep_ref, send_ref = refs[parties:]
    rows, phases = row_ids
    my_row, my_phase = lax.axis_index("row"), lax.axis_index("phase")
    block = keep_ref.shape[0] // rows
    values = jnp.concatenate([ref[0:capacity, :] for ref in arrived], axis=0)
    slots = [
        decoded(ref[capacity : capacity + CODE_ROWS, 0:capacity]) - SLOT_BASE for ref in arrived
    ]
    slots = jnp.concatenate(slots, axis=1).astype(jnp.int32)
    down = lax.broadcasted_iota(jnp.int32, (block, parties * capacity), 0)
    for other in range(phases):
        for step in range(rows):
            base = ((my_row ^ step) * phases + (my_phase ^ other)) * block
            chosen = (slots - base == down).astype(jnp.float32).astype(jnp.bfloat16)
            total = dot(chosen, values)
            if other == 0:
                keep_ref[step * block : (step + 1) * block, :] = total
            else:
                send_ref[step * block : (step + 1) * block, :] = total.astype(jnp.bfloat16)


def combine_kernel(block, kept_ref, come_ref, own_ref, *sent_refs):
    for step in range(len(sent_refs) + 1):
        part = slice(step * block, (step + 1) * block)
        total = kept_ref[part, :] + come_ref[part, :].astype(jnp.float32)
        if step == 0:
            own_ref[...] = total
        else:
            sent_refs[step - 1][...] = total.astype(jnp.bfloat16)


def finish_kernel(own_ref, *refs):
    total = own_ref[...]
    for come_ref in refs[:-2]:
        total = total + come_ref[...].astype(jnp.float32)
    refs[-1][...] = total


def loop(count, body):
    if count <= 4:
        for index in range(count):
            body(index)
    else:
        lax.fori_loop(0, count, lambda index, carry: (body(index), carry)[1], 0)


def rows_at(start, count, step):
    if isinstance(start, int):
        return pl.ds(start, count)
    return pl.ds(pl.multiple_of(start, step), count)


def tall_blocks(window):
    return window if window <= 4 else 1


def look_up(ids, pieces):
    total = None
    for base, piece in pieces:
        along = lax.broadcasted_iota(jnp.int32, (ids.shape[0], piece.shape[0]), 1)
        chosen = (along == ids - base).astype(jnp.float32).astype(jnp.bfloat16)
        part = dot(chosen, piece[...])
        total = part if total is None else total + part
    return total


def half_kernel(table_ref, half_ref):
    half = half_ref.shape[0]
    start = pl.multiple_of(lax.axis_index("phase") * half, half)
    half_ref[...] = table_ref[pl.ds(start, half), :]


def join_kernel(first_ref, second_ref, joined_ref):
    count = first_ref.shape[0]
    joined_ref[0:count, :] = first_ref[...]
    joined_ref[count:, :] = second_ref[...]


def lookup_kernel(
    window,
    ids_ref,
    lengths_ref,
    table_ref,
    near_ref,
    next_ref,
    emb_ref,
    column_ref,
    earliest_ref,
):
    my_row = lax.axis_index("row")
    my_phase = lax.axis_index("phase")
    size = ids_ref.shape[1]
    owned = table_ref.shape[0]

    def column(index):
        row = my_row - (window - 1) + index
        ids = ids_ref[pl.ds(jnp.maximum(row, 0) ^ my_row, 1), :].astype(jnp.float32)
        return as_column(jnp.where(row >= 0, ids, -1.0))

    tall = tall_blocks(window)
    height = tall * size
    pieces = ((0, table_ref), (owned, near_ref), (2 * owned, next_ref))

    def step(index):
        part = rows_at(index * height, height, size)
        ids = [column(index * tall + block) for block in range(tall)]
        ids = jnp.concatenate(ids, axis=0).astype(jnp.int32)
        emb_ref[part, :] = look_up(ids, pieces).astype(jnp.bfloat16)
        column_ref[part, :] = ids - 3 * owned
        position = (my_row - (window - 1)) * size + index * height
        position = position + lax.broadcasted_iota(jnp.int32, (height, 1), 0)
        earliest = jnp.zeros((height, 1), jnp.int32)
        bound = jnp.int32(0)
        for segment in range(lengths_ref.shape[2] - 1):
            bound = bound + lengths_ref[0, my_phase, segment]
            earliest = jnp.where(position >= bound, bound, earliest)
        earliest_ref[part, :] = earliest

    loop(window // tall, step)


def weights_kernel(proj_own, proj_other, outw_own, outw_other, proj_ref, outw_ref, sems):
    my_phase = lax.axis_index("phase")
    copies = [
        pltpu.make_async_copy(proj_own.at[0], proj_ref.at[my_phase], sems.at[0]),
        pltpu.make_async_copy(proj_other.at[0], proj_ref.at[1 - my_phase], sems.at[1]),
        pltpu.make_async_copy(outw_own.at[0], outw_ref.at[my_phase], sems.at[2]),
        pltpu.make_async_copy(outw_other.at[0], outw_ref.at[1 - my_phase], sems.at[3]),
    ]
    for copy in copies:
        copy.start()
    for copy in copies:
        copy.wait()


def section_kernel(
    window,
    earliest_ref,
    ids_ref,
    early_ref,
    far_ref,
    far2_ref,
    proj_ref,
    outw_ref,
    gain_ref,
    out_ref,
    done_ref,
    emb_ref,
    act_ref,
    mid_ref,
    mix_ref,
):
    my_row = lax.axis_index("row")
    size = out_ref.shape[0]
    half = far_ref.shape[0]
    tall = tall_blocks(window)
    height = tall * size

    def rows(start, count=height):
        return rows_at(start, count, size)

    def late(step):
        part = rows(step * height)
        found = look_up(ids_ref[part, :], ((0, far_ref), (half, far2_ref)))
        emb_ref[part, :] = early_ref[part, :].astype(jnp.float32) + found

    loop(window // tall, late)

    first_pos = (my_row - (window - 1)) * size
    across = lax.broadcasted_iota(jnp.int32, (1, size), 1)

    def attend(start, count, key_start, diagonal):
        query_pos = first_pos + start + lax.broadcasted_iota(jnp.int32, (count, 1), 0)
        key_pos = first_pos + key_start + across
        visible = key_pos >= earliest_ref[rows(start, count), :]
        if diagonal:
            visible = visible & (key_pos <= query_pos)
        for head in range(HEADS):
            cols = head * HEAD_DIM
            queries = act_ref[rows(start, count), 2 * INNER + cols : 2 * INNER + cols + HEAD_DIM]
            keys = act_ref[rows(key_start, size), 3 * INNER + cols : 3 * INNER + cols + HEAD_DIM]
            values = act_ref[rows(key_start, size), INNER + cols : INNER + cols + HEAD_DIM]
            scores = lax.dot_general(queries, keys, NT, preferred_element_type=jnp.float32)
            weights = jnp.where(visible, silu_of_half(scores), 0.0).astype(jnp.bfloat16)
            mix_ref[rows(start, count), cols : cols + HEAD_DIM] += dot(weights, values)

    def project(start, count, section, parts):
        source = emb_ref if section == 0 else mid_ref
        values = source[rows(start, count), :].astype(jnp.float32)
        normed = layer_norm(values, 0.5).astype(jnp.bfloat16)
        for part in parts:
            cols = part * INNER
            act = silu_of_half(dot(normed, proj_ref[section, :, cols : cols + INNER]))
            if part == 2:
                act = 0.5 * act
            act_ref[rows(start, count), cols : cols + INNER] = act.astype(jnp.bfloat16)

    def finish(start, count, section):
        source = emb_ref if section == 0 else mid_ref
        values = source[rows(start, count), :].astype(jnp.float32)
        gates = act_ref[rows(start, count), 0:INNER].astype(jnp.float32)
        gated = (layer_norm(mix_ref[rows(start, count), :]) * gates).astype(jnp.bfloat16)
        return values + dot(gated, outw_ref[section])

    last = (window - 1) * size
    mix_ref[...] = jnp.zeros(mix_ref.shape, jnp.float32)
    loop(window // tall, lambda step: project(step * height, height, 0, (3, 2, 1, 0)))
    if tall == window:
        for block in range(window):
            attend(block * size, height - block * size, block * size, True)
    else:

        def with_keys(block):
            attend(block * size, size, block * size, True)
            lax.fori_loop(
                block + 1,
                window,
                lambda later, c: (attend(later * size, size, block * size, False), c)[1],
                0,
            )

        loop(window, with_keys)

    def close_first(step):
        mid_ref[rows(step * height), :] = finish(step * height, height, 0).astype(jnp.bfloat16)

    loop(window // tall, close_first)
    mix_ref[last : last + size, :] = jnp.zeros((size, INNER), jnp.float32)
    loop(window // tall, lambda step: project(step * height, height, 1, (3, 1)))
    project(last, size, 1, (2, 0))
    attend(last, size, last, True)
    loop(window - 1, lambda block: attend(last, size, block * size, False))
    closing = finish(last, size, 1)
    out_ref[...] = (layer_norm(closing) * gain_ref[...]).astype(jnp.bfloat16)
    done_ref[...] = jnp.zeros(done_ref.shape, jnp.float32)


def body(
    item_table, item_owner, item_slot, seq_lengths, row_grads, proj_weight, out_weight, final_gain
):
    parties = lax.axis_size("emb")
    row_count = lax.axis_size("row")
    phases = lax.axis_size("phase")
    my_emb = lax.axis_index("emb")
    my_row = lax.axis_index("row")
    my_phase = lax.axis_index("phase")
    size = item_slot.shape[2]
    width = item_table.shape[1]
    owned = item_table.shape[0]
    half = owned // 2
    capacity = max(16, 2 * size // parties)
    window = -(-3 * row_count // 4)
    vmem = pltpu.MemorySpace.VMEM
    smem = pltpu.MemorySpace.SMEM

    def params(mebibytes):
        return pltpu.CompilerParams(vmem_limit_bytes=mebibytes * 1024 * 1024)

    def across(shard, first):
        pairs = []
        for emb in range(parties):
            for phase in range(phases):
                by = 1 if (phase == 0) == first else 2
                pairs.append((emb * phases + phase, (emb ^ by) * phases + phase))
        return lax.ppermute(shard, ("emb", "phase"), pairs)

    proj_other = exchanged(proj_weight, "phase", 1)
    outw_other = exchanged(out_weight, "phase", 1)

    on_chip = pl.BlockSpec(memory_space=vmem)
    scalars = pl.BlockSpec(memory_space=smem)
    anywhere = pl.BlockSpec(memory_space=pl.ANY)

    def array(rows, dtype=jnp.bfloat16):
        return jax.ShapeDtypeStruct((rows, width), dtype)

    owners, slots = item_owner.reshape(1, size), item_slot.reshape(1, size)
    *packed, ids = pl.pallas_call(
        functools.partial(pack_kernel, parties, capacity, owned),
        out_shape=[array(capacity + CODE_ROWS)] * parties
        + [jax.ShapeDtypeStruct((1, size), jnp.int32)],
        in_specs=[on_chip] * 3,
        out_specs=[on_chip] * (parties + 1),
        compiler_params=params(4),
        name="pack",
    )(owners, slots, row_grads.reshape(size, width))
    away = {by: exchanged(packed[by], "emb", by) for by in range(parties - 1, 0, -1)}
    arrived = [packed[0]] + [away[by] for by in range(parties - 1, 0, -1)]
    near = across(item_table, True)
    by = 1
    while by < row_count:
        ids = pl.pallas_call(
            join_kernel,
            out_shape=jax.ShapeDtypeStruct((2 * by, size), jnp.int32),
            in_specs=[on_chip] * 2,
            out_specs=on_chip,
            compiler_params=params(4),
            name="join",
        )(ids, exchanged(ids, "row", by))
        by *= 2
    near, ids = lax.optimization_barrier((near, ids))
    following = exchanged(near, "phase", 1)
    near_half = pl.pallas_call(
        half_kernel,
        out_shape=array(half),
        in_specs=[on_chip],
        out_specs=on_chip,
        compiler_params=params(4),
        name="half",
    )(near)
    far = across(near_half, False)
    ids, *arrived = lax.optimization_barrier((ids, *arrived))
    block = owned // (row_count * phases)
    count = row_count * block
    kept, sent = pl.pallas_call(
        functools.partial(scatter_kernel, parties, capacity, (row_count, phases)),
        out_shape=[array(count, jnp.float32), array(count)],
        in_specs=[on_chip] * parties,
        out_specs=[on_chip] * 2,
        compiler_params=params(4),
        cost_estimate=pl.CostEstimate(flops=32999999999, bytes_accessed=0, transcendentals=0),
        name="scatter",
    )(*arrived)
    come = exchanged(sent, "phase", 1)
    own, *sent = pl.pallas_call(
        functools.partial(combine_kernel, block),
        out_shape=[array(block, jnp.float32)] + [array(block)] * (row_count - 1),
        in_specs=[on_chip] * 2,
        out_specs=[on_chip] * row_count,
        compiler_params=params(4),
        name="combine",
    )(kept, come)
    sums = [exchanged(sent[by - 1], "row", by) for by in range(1, row_count)]

    early, columns, earliest = pl.pallas_call(
        functools.partial(lookup_kernel, window),
        out_shape=[
            array(window * size),
            jax.ShapeDtypeStruct((window * size, 1), jnp.int32),
            jax.ShapeDtypeStruct((window * size, 1), jnp.int32),
        ],
        in_specs=[on_chip, scalars] + [on_chip] * 3,
        out_specs=[on_chip] * 3,
        compiler_params=params(8 + window),
        name="lookup",
    )(ids, seq_lengths, item_table, near, following)
    proj_both, outw_both = pl.pallas_call(
        weights_kernel,
        out_shape=[
            jax.ShapeDtypeStruct((2,) + proj_weight.shape[1:], jnp.bfloat16),
            jax.ShapeDtypeStruct((2,) + out_weight.shape[1:], jnp.bfloat16),
        ],
        in_specs=[anywhere] * 4,
        out_specs=[on_chip] * 2,
        scratch_shapes=[pltpu.SemaphoreType.DMA((4,))],
        compiler_params=params(8),
        name="weights",
    )(proj_weight, proj_other, out_weight, outw_other)
    far, early, outw_both = lax.optimization_barrier((far, early, outw_both))
    far2 = exchanged(far, "phase", 1)
    states, done = pl.pallas_call(
        functools.partial(section_kernel, window),
        out_shape=[array(size), jax.ShapeDtypeStruct((8, 128), jnp.float32)],
        in_specs=[on_chip] * 8,
        out_specs=[on_chip] * 2,
        scratch_shapes=[
            pltpu.VMEM((window * size, width), jnp.float32),
            pltpu.VMEM((window * size, 4 * INNER), jnp.bfloat16),
            pltpu.VMEM((window * size, width), jnp.bfloat16),
            pltpu.VMEM((window * size, INNER), jnp.float32),
        ],
        compiler_params=params(10 + 4 * window),
        cost_estimate=pl.CostEstimate(flops=1, bytes_accessed=1, transcendentals=0),
        name="sections",
    )(
        earliest,
        columns,
        early,
        far,
        far2,
        proj_both,
        outw_both,
        final_gain.reshape(1, width),
    )
    table_grad = pl.pallas_call(
        finish_kernel,
        out_shape=array(block, jnp.float32),
        in_specs=[on_chip] * row_count + [anywhere],
        out_specs=on_chip,
        compiler_params=params(4),
        name="finish",
    )(own, *sums, done)
    return (states.reshape(1, 1, size, width), table_grad)


def solution(mesh):
    placed = (
        P("emb", None),
        P("emb", "phase", "row", None),
        P("emb", "phase", "row"),
        P("emb", None, None),
        P("emb", "phase", "row", None),
        P("phase", None, None),
        P("phase", None, None),
        P(),
    )
    return jax.shard_map(
        body,
        mesh=mesh,
        in_specs=placed,
        out_specs=(P("emb", "phase", "row", None), P(("emb", "row", "phase"), None)),
        check_vma=False,
    )
```
